128 devices in a mesh: fsdp: 8 (over y, z_lo), tensor: 16 (over x, z_hi, core).
Axes of the slice: x: 4, y: 4, z: 4 (z_hi: 2, z_lo: 2; z = z_hi * 2 + z_lo), core: 2. Of those that a mesh axis runs over, the one named last changes fastest.
Arguments:
- inputs: bfloat16 [16384, 2048], P(('fsdp', 'tensor')), may hold values from -40 to 40
- gain: float32 [2048], replicated, may hold values from 0.1 to 1.9
- w_query: bfloat16 [2048, 4096], P('fsdp', 'tensor'), may hold values from -0.046875 to 0.046875
- w_key: bfloat16 [2048, 4096], P('fsdp', 'tensor'), may hold values from -0.046875 to 0.046875
- w_value: bfloat16 [2048, 4096], P('fsdp', 'tensor'), may hold values from -0.125 to 0.125
- w_out: bfloat16 [2048, 4096], P('fsdp', 'tensor'), may hold values from -0.125 to 0.125
- rel_bias: float32 [64, 32], P('tensor'), may hold values from -4 to 260
- d_output: bfloat16 [16384, 2048], P(('fsdp', 'tensor')), may hold values from -24 to 24
Outputs:
- d_inputs: bfloat16 [16384, 2048], P(('fsdp', 'tensor'))
- grad_query: float32 [2048, 4096], P('fsdp', 'tensor')
- grad_key: float32 [2048, 4096], P('fsdp', 'tensor')
- grad_value: float32 [2048, 4096], P('fsdp', 'tensor')
- grad_out: float32 [2048, 4096], P('fsdp', 'tensor')
The draws below stay inside these ranges and needn't reach their ends.
All inputs are finite; a program needn't handle non-finite values.
Results may differ from the reference program's by a relative error of at most 0.017.
Values may be sent and summed in bfloat16 or wider, within the bound.
A program may use at most 128 MiB of HBM per device.

```python
import jax
import jax.numpy as jnp
import numpy as np
from jax import lax

D = 2048
HEADS = 64
HEAD_DIM = 64
BUCKETS = 32
MAX_DIST = 128
LEN = 256
PASS_ROW = 8
INNER = 4096
PASS = 64
N_FSDP = 8
N_TENSOR = 16


def draw_inputs(key, part):
    key = jax.random.fold_in(key, 11)
    raw_key, row_key, col_key = jax.random.split(key, 3)
    col_scale = jnp.exp(jax.random.uniform(col_key, (D,), jnp.float32) * jnp.log(10.0))
    raw_values = jnp.clip(jax.random.normal(raw_key, (PASS * LEN, D), jnp.float32), -4.0, 4.0)
    row_scale = jnp.exp(jax.random.uniform(row_key, (PASS * LEN, 1), jnp.float32) * jnp.log(10.0))
    return (0.1 * raw_values * row_scale * col_scale).astype(jnp.bfloat16)


def draw_rel_bias(key, part):
    key = jax.random.fold_in(key, 23)
    raw_key = jax.random.fold_in(key, 0)
    return jnp.clip(jax.random.normal(raw_key, (HEADS, BUCKETS), jnp.float32), -4.0, 4.0)


def with_spikes(result, key, source, target, parts, factor):
    def block_of(dim):
        return (jnp.arange(result.shape[dim]) // (result.shape[dim] // parts)).reshape((-1,) + (1,) * (result.ndim - 1 - dim))

    one_side = jax.random.permutation(key, parts)[block_of(target)]
    far = (block_of(target) + parts // 2) % parts
    return jnp.where((block_of(source) == one_side) | (block_of(source) == far), factor * result, result)


def shard_levels(rng, shape, pieces, low, top_value):
    def one(axis_at, shards_of):
        steps = jax.random.uniform(jax.random.fold_in(jax.random.fold_in(rng, 6), axis_at), (shards_of,), jnp.float32, low / len(pieces), top_value / len(pieces))
        return jnp.repeat(jnp.exp(steps), shape[axis_at] // shards_of).reshape((-1,) + (1,) * (len(shape) - axis_at - 1))

    level = one(*pieces[0])
    for cut in pieces[1:]:
        level = level * one(*cut)
    return level


def scatter_about(stream_key, extent, scale, reach, cuts=(), dtype=jnp.bfloat16):
    drawn = jax.random.normal(stream_key, extent, jnp.float32) * scale
    if len(cuts) > 0:
        drawn = shard_levels(stream_key, extent, cuts, -0.22, 0.18) * drawn
    return jnp.clip(drawn, min=-reach, max=reach).astype(dtype)


def noise_with(own_key, shape, scale, limit, cuts, heavy, dtype=jnp.bfloat16):
    values = scale * jax.random.normal(own_key, shape, jnp.float32)
    if cuts:
        values = values * shard_levels(own_key, shape, cuts, -0.22, 0.18)
    return jnp.clip(with_spikes(values, jax.random.fold_in(own_key, 3), *heavy), -limit, limit).astype(dtype)


def setup_inputs(seed: int = 0) -> dict:
    keys = jax.random.split(jax.random.key(seed), 9)
    return {
        "inputs": draw_inputs(jax.random.fold_in(keys[8], 71), 0),
        "gain": jnp.clip(1.0 + 0.18 * jax.random.normal(keys[1], (D,), jnp.float32), 0.1, 1.9),
        "w_query": scatter_about(keys[2], (D, INNER), (8 * D) ** -0.5, 0.046875, ((0, 8), (1, 16))),
        "w_key": scatter_about(keys[3], (D, INNER), (8 * D) ** -0.5, 0.046875, ((0, 8), (1, 16))),
        "w_value": scatter_about(keys[4], (D, INNER), D ** -0.5, 0.125, ((0, 8), (1, 16))),
        "w_out": scatter_about(keys[5], (D, INNER), D ** -0.5, 0.125, ((0, 8), (1, 16))),
        "rel_bias": draw_rel_bias(jax.random.fold_in(keys[8], 71), 0),
        "d_output": noise_with(keys[7], (PASS * LEN, D), 1.0, 24.0, ((0, 128),), (0, 1, 128, 5.5)),
    }


epsilon = 1e-06

def bucket_grid(length, buckets, max_distance):
    positions = np.arange(length)
    relative = positions[None, :] - positions[:, None]
    half_count = buckets // 2
    exact_count = half_count // 2
    side_offset = np.where(relative > 0, half_count, 0)
    distance = np.abs(relative)
    log_ratio = np.log(np.maximum(distance, 1) / exact_count) / np.log(max_distance / exact_count)
    far_bucket = np.minimum(exact_count + np.floor(log_ratio * (half_count - exact_count)).astype(np.int64), half_count - 1)
    return (side_offset + np.where(distance < exact_count, distance, far_bucket)).astype(np.int32)

def bias_grid(rel_bias, bucket_ids):
    expanded = jnp.zeros((rel_bias.shape[0],) + bucket_ids.shape, jnp.float32)
    for bucket in range(rel_bias.shape[1]):
        chosen = jnp.asarray(bucket_ids == bucket, jnp.float32)
        expanded = expanded + rel_bias[:, bucket][:, None, None] * chosen[None]
    return expanded

def rounded(array):
    return lax.optimization_barrier(array.astype(jnp.bfloat16))

def row_pass(inputs, d_output, gain, w_query, w_key, w_value, w_out, bias_full):
    length, rows_pass, width = inputs.shape
    inner = w_query.shape[1]
    flat_in = inputs.astype(jnp.float32)
    inv_rms = lax.rsqrt(lax.optimization_barrier(jnp.mean(flat_in * flat_in, axis=-1, keepdims=True)) + epsilon)
    unit_rows = flat_in * inv_rms
    normed = (unit_rows * gain).astype(jnp.bfloat16)
    normed_flat = normed.reshape(length * rows_pass, width)

    def project(weight):
        return rounded(jnp.dot(normed_flat, weight, preferred_element_type=jnp.float32))

    def heads_view(array):
        return array.reshape(length, rows_pass, HEADS, HEAD_DIM).astype(jnp.float32)
    query_rows = project(w_query)
    key_rows = project(w_key)
    value_rows = project(w_value)
    scores = jnp.einsum('iphe,jphe->phij', heads_view(query_rows), heads_view(key_rows)) + bias_full[None]
    row_max = lax.optimization_barrier(jnp.max(scores, axis=-1, keepdims=True))
    exp_scores = jnp.exp(scores - row_max)
    attn_probs = exp_scores / lax.optimization_barrier(jnp.sum(exp_scores, axis=-1, keepdims=True))
    probs_half = rounded(attn_probs).astype(jnp.float32)
    context = rounded(jnp.einsum('phij,jphe->iphe', probs_half, heads_view(value_rows)))
    context_flat = context.reshape(length * rows_pass, inner)
    cot_flat = d_output.reshape(length * rows_pass, width)
    d_context = rounded(jnp.dot(cot_flat, w_out, preferred_element_type=jnp.float32))
    out_term = jnp.dot(cot_flat.T, context_flat, preferred_element_type=jnp.float32)
    d_heads = heads_view(d_context)
    d_prob = jnp.einsum('iphe,jphe->phij', d_heads, heads_view(value_rows))
    d_value = rounded(jnp.einsum('phij,iphe->jphe', probs_half, d_heads)).reshape(length * rows_pass, inner)
    row_dot = lax.optimization_barrier(jnp.sum(attn_probs * d_prob, axis=-1, keepdims=True))
    d_score = rounded(attn_probs * (d_prob - row_dot)).astype(jnp.float32)
    d_query = rounded(jnp.einsum('phij,jphe->iphe', d_score, heads_view(key_rows))).reshape(length * rows_pass, inner)
    d_key = rounded(jnp.einsum('phij,iphe->jphe', d_score, heads_view(query_rows))).reshape(length * rows_pass, inner)
    group_width = inner // N_TENSOR

    def group_view(array):
        return array.reshape(array.shape[0], N_TENSOR, group_width).transpose(1, 0, 2)

    def add_group(running, slices):
        grad_q, grad_k, grad_v, weight_q, weight_k, weight_v = slices
        term_sum = jnp.dot(grad_q, weight_q.T, preferred_element_type=jnp.float32)
        term_sum = term_sum + jnp.dot(grad_k, weight_k.T, preferred_element_type=jnp.float32)
        term_sum = term_sum + jnp.dot(grad_v, weight_v.T, preferred_element_type=jnp.float32)
        return (running + rounded(term_sum).astype(jnp.float32), None)
    stacked = (group_view(d_query), group_view(d_key), group_view(d_value), group_view(w_query), group_view(w_key), group_view(w_value))
    d_normed, _ = lax.scan(add_group, jnp.zeros((length * rows_pass, width), jnp.float32), stacked)

    def weight_term(left, right):
        return rounded(jnp.dot(left.T, right, preferred_element_type=jnp.float32)).astype(jnp.float32)
    grads = (weight_term(normed_flat, d_query), weight_term(normed_flat, d_key), weight_term(normed_flat, d_value), rounded(out_term).astype(jnp.float32))
    d_unit = d_normed.reshape(length, rows_pass, width) * gain
    branch = inv_rms * (d_unit - unit_rows * lax.optimization_barrier(jnp.mean(d_unit * unit_rows, axis=-1, keepdims=True)))
    d_inputs = (d_output.astype(jnp.float32) + branch).astype(jnp.bfloat16)
    return (d_inputs, grads)

def reference(inputs, gain, w_query, w_key, w_value, w_out, rel_bias, d_output):
    bias_full = bias_grid(rel_bias, bucket_grid(LEN, BUCKETS, MAX_DIST))

    def row_view(array):
        return array.reshape(N_FSDP, PASS_ROW, LEN, D).transpose(0, 2, 1, 3)

    def row_step(grad_sums, blocks):
        in_rows, cot_rows = blocks
        d_rows, grads = row_pass(in_rows, cot_rows, gain, w_query, w_key, w_value, w_out, bias_full)
        return (tuple((total + extra for total, extra in zip(grad_sums, grads))), d_rows)
    zero_grad = jnp.zeros((D, INNER), jnp.float32)
    grad_sums, d_rows = lax.scan(row_step, (zero_grad, zero_grad, zero_grad, zero_grad), (row_view(inputs), row_view(d_output)))
    d_inputs = d_rows.transpose(0, 2, 1, 3).reshape(PASS * LEN, D)
    return (d_inputs, grad_sums[0], grad_sums[1], grad_sums[2], grad_sums[3])
```

```python
import functools

import jax
import jax.numpy as jnp
import numpy as np
from jax import lax
from jax.experimental import pallas as pl
from jax.experimental.pallas import tpu as pltpu
from jax.sharding import PartitionSpec as P

BUCKETS = 32
MAX_DIST = 128
LEN = 256
EPSILON = 1e-06
MESH = pl.DeviceIdType.MESH
BF = jnp.bfloat16
F32 = jnp.float32
OUT, VAL, QRY, KEY = 0, 1, 2, 3


def bucket_steps():
    half_count = BUCKETS // 2
    exact_count = half_count // 2
    distance = np.arange(LEN)
    log_ratio = np.log(np.maximum(distance, 1) / exact_count) / np.log(MAX_DIST / exact_count)
    far = np.minimum(
        exact_count + np.floor(log_ratio * (half_count - exact_count)).astype(np.int64),
        half_count - 1,
    )
    bucket = np.where(distance < exact_count, distance, far)
    return [int(np.argmax(bucket >= k)) for k in range(half_count)]


def dot_nn(a, b):
    return lax.dot_general(a, b, (((1,), (0,)), ((), ())), preferred_element_type=F32)


def dot_nt(a, b):
    return lax.dot_general(a, b, (((1,), (1,)), ((), ())), preferred_element_type=F32)


class Links:
    def __init__(self, send_sem, recv_sem):
        self.send_sem, self.recv_sem = send_sem, recv_sem
        self.copies = {}

    def start(self, key, src, dst, peer):
        k = len(self.copies)
        copy = pltpu.make_async_remote_copy(
            src_ref=src,
            dst_ref=dst,
            send_sem=self.send_sem.at[k],
            recv_sem=self.recv_sem.at[k],
            device_id=peer,
            device_id_type=MESH,
        )
        copy.start()
        self.copies[key] = copy

    def arrived(self, *key):
        self.copies[key].wait_recv()

    def finish(self):
        for copy in self.copies.values():
            copy.wait_send()


N_COPIES = 136


def kernel(
    x_ref, gain_ref, wq_ref, wk_ref, wv_ref, wo_ref, rb_ref, do_ref,
    dx_ref, gq_ref, gk_ref, gv_ref, go_ref,
    tok, cot, wgt, rel, bias, heads, dheads, rows_t, part, sum1y, sum1z, sum2, dn, dn_sib, dn_x,
    splat, send_sem, recv_sem,
):
    f, t = lax.axis_index("fsdp"), lax.axis_index("tensor")
    x, zh, c = t // 4, (t // 2) % 2, t % 2
    y, zl = f // 2, f % 2
    z = zh * 2 + zl

    def dev(x, y, z, c):
        return (y * 2 + z % 2, (x * 2 + z // 2) * 2 + c)

    def xp(k):
        return (x + k) % 4

    def yp(k):
        return (y + k) % 4

    def zp(k):
        return (z + k) % 4

    sib = dev(x, y, z, 1 - c)
    to_x = {k: dev(xp(k), y, z, c) for k in (1, 2, 3)}
    to_y = {k: dev(x, yp(k), z, c) for k in (1, 2, 3)}
    to_z = {k: dev(x, y, zp(k), c) for k in (1, 2, 3)}
    peers = [sib] + list(to_x.values()) + list(to_y.values()) + list(to_z.values())
    barrier = pltpu.get_barrier_semaphore()
    for peer in peers:
        pl.semaphore_signal(barrier, inc=1, device_id=peer, device_id_type=MESH)
    pl.semaphore_wait(barrier, len(peers))

    net = Links(send_sem, recv_sem)

    def w_y(w, yy, zz, row, n):
        return wgt.at[w, zz // 2, yy, zz % 2, pl.ds(row, n)]

    def w_ycol(w, zz, row, n):
        return wgt.at[w, zz // 2, pl.ds(0, 4), zz % 2, pl.ds(row, n)]

    def w_zrow(w, yy, row, n):
        return wgt.at[w, pl.ds(0, 2), yy, pl.ds(0, 2), pl.ds(row, n)]

    for w, ref in ((OUT, wo_ref), (VAL, wv_ref), (QRY, wq_ref), (KEY, wk_ref)):
        wgt[w, zh, y, zl] = ref[...]
    rel[zh] = jnp.zeros((8, 128), F32)
    rel[zh, 0:4, 0:32] = rb_ref[...]
    cot[x, c] = do_ref[...]
    net.start(("rel",), rel.at[zh], rel.at[zh], to_z[2])

    def spread_own(name, buf):
        own = buf.at[x, c]
        net.start((name, 1), own, own, to_x[1])
        net.start((name, 3), own, own, to_x[3])
        net.start((name, "sib", 0), own, own, sib)

    spread_own("cot", cot)
    for w in range(4):
        a, b = w_y(w, y, z, 0, 128), w_y(w, y, z, 128, 128)
        net.start(("y", w, 1), a, a, to_y[1])
        net.start(("y", w, 3), a, a, to_y[3])
        net.start(("z", w, 1), b, b, to_z[1])
        net.start(("z", w, 3), b, b, to_z[3])

    def norm_rows(k):
        rows = x_ref[pl.ds(pl.multiple_of(k * 16, 16), 16), :].astype(F32)
        inv = lax.rsqrt(jnp.mean(rows * rows, axis=-1, keepdims=True) + EPSILON)
        return rows * inv, inv

    @pl.loop(0, 8)
    def _(k):
        unit, _ = norm_rows(k)
        tok[x, c, pl.ds(pl.multiple_of(k * 16, 16), 16), :] = (unit * gain_ref[...]).astype(BF)

    spread_own("tok", tok)

    for w in range(4):
        net.arrived("y", w, 1)
        s = w_y(w, yp(3), z, 0, 64)
        net.start(("yf", w, 1), s, s, to_y[1])
        net.arrived("z", w, 1)
        s = w_y(w, y, zp(3), 128, 64)
        net.start(("zf", w, 1), s, s, to_z[1])
        net.arrived("y", w, 3)
        s = w_y(w, yp(1), z, 64, 64)
        net.start(("yf", w, 3), s, s, to_y[3])
        net.arrived("z", w, 3)
        s = w_y(w, y, zp(1), 192, 64)
        net.start(("zf", w, 3), s, s, to_z[3])

    for w in range(4):
        net.arrived("yf", w, 1)
        net.arrived("yf", w, 3)
        s = w_ycol(w, z, 0, 128)
        net.start(("z2", w, 1), s, s, to_z[1])
        net.start(("z2", w, 3), s, s, to_z[3])
        net.arrived("zf", w, 1)
        net.arrived("zf", w, 3)
        s = w_zrow(w, y, 128, 128)
        net.start(("y2", w, 1), s, s, to_y[1])
        net.start(("y2", w, 3), s, s, to_y[3])

    net.arrived("rel")
    steps = bucket_steps()
    table = jnp.concatenate([rel[0, 0:4, :], rel[1, 0:4, :]], axis=0)
    for k in range(BUCKETS):
        splat[k] = jnp.broadcast_to(table[:, k : k + 1], (8, 128))

    @pl.loop(0, LEN // 8)
    def _(k):
        i = lax.broadcasted_iota(jnp.int32, (8, LEN), 0) + k * 8
        r = lax.broadcasted_iota(jnp.int32, (8, LEN), 1) - i
        values = [None] * 8

        def row(b, h):
            return jnp.broadcast_to(splat[b, h : h + 1, 0:1], (8, LEN))

        for h in range(8):
            values[h] = row(0, h)
        for b in range(1, BUCKETS // 2):
            chosen = r <= -steps[b]
            for h in range(8):
                values[h] = jnp.where(chosen, row(b, h), values[h])
        for b in range(1, BUCKETS // 2):
            chosen = r >= steps[b]
            for h in range(8):
                values[h] = jnp.where(chosen, row(BUCKETS // 2 + b, h), values[h])
        for h in range(8):
            bias[h, pl.ds(pl.multiple_of(k * 8, 8), 8), :] = values[h]

    def pass_tokens(name, buf):
        net.arrived(name, 1)
        s = buf.at[xp(3), c, pl.ds(0, 64)]
        net.start((name, "f", 1), s, s, to_x[1])
        s = buf.at[xp(3), c]
        net.start((name, "sib", 3), s, s, sib)
        net.arrived(name, 3)
        s = buf.at[xp(1), c, pl.ds(64, 64)]
        net.start((name, "f", 3), s, s, to_x[3])
        s = buf.at[xp(1), c]
        net.start((name, "sib", 1), s, s, sib)

    def pass_far(name, buf):
        net.arrived(name, "f", 1)
        net.arrived(name, "f", 3)
        s = buf.at[xp(2), c]
        net.start((name, "sib", 2), s, s, sib)

    def tokens_here(name):
        for k in range(4):
            net.arrived(name, "sib", k)

    def pass_weight(w):
        net.arrived("z2", w, 1)
        s = w_ycol(w, zp(3), 0, 64)
        net.start(("z2f", w, 1), s, s, to_z[1])
        net.arrived("y2", w, 1)
        s = w_zrow(w, yp(3), 128, 64)
        net.start(("y2f", w, 1), s, s, to_y[1])
        net.arrived("z2", w, 3)
        s = w_ycol(w, zp(1), 64, 64)
        net.start(("z2f", w, 3), s, s, to_z[3])
        net.arrived("y2", w, 3)
        s = w_zrow(w, yp(1), 192, 64)
        net.start(("y2f", w, 3), s, s, to_y[3])

    def weight_here(w):
        for name in ("z2f", "y2f"):
            net.arrived(name, w, 1)
            net.arrived(name, w, 3)

    def project(w, buf):
        @pl.loop(0, 4)
        def _(k):
            m, g = k // 2, k % 2
            left = buf[pl.ds(m * 2, 2)].reshape(512, 2048)
            right = wgt[w, g].reshape(2048, 256)
            heads[w, g, pl.ds(pl.multiple_of(m * 512, 512), 512), :] = dot_nn(left, right).astype(BF)

    pass_weight(OUT)
    pass_tokens("cot", cot)
    pass_weight(VAL)
    pass_tokens("tok", tok)
    pass_weight(QRY)
    pass_far("cot", cot)
    tokens_here("cot")
    weight_here(OUT)
    project(OUT, cot)
    pass_far("tok", tok)
    pass_weight(KEY)
    tokens_here("tok")
    weight_here(VAL)
    project(VAL, tok)
    weight_here(QRY)
    project(QRY, tok)
    weight_here(KEY)
    project(KEY, tok)

    lane = lax.broadcasted_iota(jnp.int32, (1, 128), 1)
    mask = [(lane < 64).astype(F32).astype(BF), (lane >= 64).astype(F32).astype(BF)]
    line = lax.broadcasted_iota(jnp.int32, (128, 1), 0)
    mask_t = [(line < 64).astype(F32).astype(BF), (line >= 64).astype(F32).astype(BF)]

    def attention(u):
        @pl.loop(0, 8)
        def _(k):
            p, g = k // 2, k % 2
            rows = pl.ds(pl.multiple_of(p * 256, 256), 256)
            lanes = pl.ds(u * 128, 128)
            dc2, v2, q2, k2 = (heads[w, g, rows, lanes] for w in range(4))
            probs_b, d_score = [], []
            for h in range(2):
                s = dot_nt(q2 * mask[h], k2) + bias[g * 4 + u * 2 + h]
                e = jnp.exp(s - jnp.max(s, axis=-1, keepdims=True))
                probs = e * (1.0 / jnp.sum(e, axis=-1, keepdims=True))
                d_prob = dot_nt(dc2 * mask[h], v2)
                row_dot = jnp.sum(probs * d_prob, axis=-1, keepdims=True)
                probs_b.append(probs.astype(BF))
                d_score.append((probs * (d_prob - row_dot)).astype(BF))
            ctx = dot_nn(
                jnp.concatenate(probs_b, axis=1),
                jnp.concatenate([v2 * mask[0], v2 * mask[1]], axis=0),
            ).astype(BF)
            dq = dot_nn(
                jnp.concatenate(d_score, axis=1),
                jnp.concatenate([k2 * mask[0], k2 * mask[1]], axis=0),
            ).astype(BF)
            dc_t, q_t = dc2.T, q2.T
            dv_t = dot_nn(
                jnp.concatenate([dc_t * mask_t[0], dc_t * mask_t[1]], axis=1),
                jnp.concatenate(probs_b, axis=0),
            ).astype(BF)
            dk_t = dot_nn(
                jnp.concatenate([q_t * mask_t[0], q_t * mask_t[1]], axis=1),
                jnp.concatenate(d_score, axis=0),
            ).astype(BF)
            cols = pl.ds(pl.multiple_of(p * 256, 256), 256)
            rows_t[u, OUT, g, :, cols] = ctx.T
            rows_t[u, VAL, g, :, cols] = dv_t
            rows_t[u, QRY, g, :, cols] = dq.T
            rows_t[u, KEY, g, :, cols] = dk_t
            dheads[VAL - 1, g, rows, lanes] = dv_t.T
            dheads[QRY - 1, g, rows, lanes] = dq
            dheads[KEY - 1, g, rows, lanes] = dk_t.T

    def weight_grads(u):
        @pl.loop(0, 8)
        def _(k):
            fy, fz = k // 2, k % 2
            cols = pl.ds(pl.multiple_of(k * 256, 256), 256)
            right = cot[:, :, :, cols].reshape(1024, 256)
            res = dot_nn(rows_t[u, OUT].reshape(256, 1024), right).astype(BF)
            part[u, OUT, :, fy, fz] = res.reshape(2, 128, 256)
            right = tok[:, :, :, cols].reshape(1024, 256)
            res = dot_nn(rows_t[u, 1:4].reshape(768, 1024), right).astype(BF)
            part[u, pl.ds(1, 3), :, fy, fz] = res.reshape(3, 2, 128, 256)

    def first_send(u, w):
        for j, k in enumerate((2, 1, 3)):
            if w in (OUT, VAL):
                src = part.at[u, w, pl.ds(0, 2), yp(k)]
                net.start(("s1", u, w, k), src, sum1y.at[u, w, j], to_y[k])
            else:
                src = part.at[u, w, zp(k) // 2, pl.ds(0, 4), zp(k) % 2]
                net.start(("s1", u, w, k), src, sum1z.at[u, w - 2, j], to_z[k])

    def first_sum(u, w):
        for k in (2, 1, 3):
            net.arrived("s1", u, w, k)
        for b in range(4):
            if w in (OUT, VAL):
                at = (u, w, b // 2, y, b % 2)
            else:
                at = (u, w, zh, b, zl)
            total = part[at].astype(F32)
            for j in range(3):
                other = sum1y[u, w, j, b // 2, b % 2] if w in (OUT, VAL) else sum1z[u, w - 2, j, b]
                total = total + other.astype(F32)
            part[at] = total.astype(BF)
        for j, k in enumerate((2, 1, 3)):
            if w in (OUT, VAL):
                src = part.at[u, w, zp(k) // 2, y, zp(k) % 2]
                net.start(("s2", u, w, k), src, sum2.at[u, w, j], to_z[k])
            else:
                src = part.at[u, w, zh, yp(k), zl]
                net.start(("s2", u, w, k), src, sum2.at[u, w, j], to_y[k])

    def second_sum(u, w, out):
        for k in (2, 1, 3):
            net.arrived("s2", u, w, k)
        total = part[u, w, zh, y, zl].astype(F32)
        for j in range(3):
            total = total + sum2[u, w, j].astype(F32)
        out[:, u * 128 : u * 128 + 128] = total.T

    attention(0)
    weight_grads(0)
    for w in range(4):
        first_send(0, w)
    attention(1)

    for k in (2, 1, 3, 0):
        p = xp(k)

        @pl.loop(0, 4)
        def _(n):
            left = [dheads[w, g, pl.ds(pl.multiple_of(p * 256, 256), 256), :] for w in range(3) for g in range(2)]
            right = [wgt[w + 1, g, n].reshape(512, 256) for w in range(3) for g in range(2)]
            total = dot_nt(left[0], right[0])
            for a, b in zip(left[1:], right[1:]):
                total = total + dot_nt(a, b)
            cols = pl.ds(pl.multiple_of(n * 512, 512), 512)
            dn[p, :, :, cols] = total.astype(BF).reshape(2, 128, 512)

        net.start(("dsib", k), dn.at[p, 1 - c], dn_sib.at[p], sib)

    weight_grads(1)
    for w in range(4):
        first_send(1, w)

    for k in (2, 1, 3, 0):
        p = xp(k)
        net.arrived("dsib", k)

        @pl.loop(0, 8)
        def _(m):
            rows = pl.ds(pl.multiple_of(m * 16, 16), 16)
            dn[p, c, rows, :] = (dn[p, c, rows, :].astype(F32) + dn_sib[p, rows, :].astype(F32)).astype(BF)

        if k:
            net.start(("dx", k), dn.at[p, c], dn_x.at[k - 1], to_x[k])

    outs = (go_ref, gv_ref, gq_ref, gk_ref)
    for u in range(2):
        for w in range(4):
            first_sum(u, w)
    for k in (2, 1, 3):
        net.arrived("dx", k)

    @pl.loop(0, 8)
    def _(m):
        rows = pl.ds(pl.multiple_of(m * 16, 16), 16)
        unit, inv = norm_rows(m)
        d_normed = dn[x, c, rows, :].astype(F32)
        for j in range(3):
            d_normed = d_normed + dn_x[j, rows, :].astype(F32)
        d_unit = d_normed * gain_ref[...]
        branch = inv * (d_unit - unit * jnp.mean(d_unit * unit, axis=-1, keepdims=True))
        dx_ref[rows, :] = (do_ref[rows, :].astype(F32) + branch).astype(BF)

    for u in range(2):
        for w in range(4):
            second_sum(u, w, outs[w])
    net.finish()


def per_device(inputs, gain, w_query, w_key, w_value, w_out, rel_bias, d_output):
    vmem = pl.BlockSpec(memory_space=pltpu.VMEM)
    grad = jax.ShapeDtypeStruct((256, 256), F32)
    return pl.pallas_call(
        kernel,
        out_shape=(jax.ShapeDtypeStruct((128, 2048), BF), grad, grad, grad, grad),
        in_specs=[vmem] * 8,
        out_specs=(vmem,) * 5,
        scratch_shapes=[
            pltpu.VMEM((4, 2, 128, 2048), BF),
            pltpu.VMEM((4, 2, 128, 2048), BF),
            pltpu.VMEM((4, 2, 4, 2, 256, 256), BF),
            pltpu.VMEM((2, 8, 128), F32),
            pltpu.VMEM((8, 256, 256), F32),
            pltpu.VMEM((4, 2, 1024, 256), BF),
            pltpu.VMEM((3, 2, 1024, 256), BF),
            pltpu.VMEM((2, 4, 2, 128, 1024), BF),
            pltpu.VMEM((2, 4, 2, 4, 2, 128, 256), BF),
            pltpu.VMEM((2, 2, 3, 2, 2, 128, 256), BF),
            pltpu.VMEM((2, 2, 3, 4, 128, 256), BF),
            pltpu.VMEM((2, 4, 3, 128, 256), BF),
            pltpu.VMEM((4, 2, 128, 2048), BF),
            pltpu.VMEM((4, 128, 2048), BF),
            pltpu.VMEM((3, 128, 2048), BF),
            pltpu.VMEM((32, 8, 128), F32),
            pltpu.SemaphoreType.DMA((N_COPIES,)),
            pltpu.SemaphoreType.DMA((N_COPIES,)),
        ],
        compiler_params=pltpu.CompilerParams(
            collective_id=0, has_side_effects=True, vmem_limit_bytes=62 * 1024 * 1024
        ),
        name="attention_backward",
    )(inputs, gain.reshape(1, -1), w_query, w_key, w_value, w_out, rel_bias, d_output)


def solution(mesh):
    return jax.shard_map(
        per_device,
        mesh=mesh,
        in_specs=(
            P(("fsdp", "tensor"), None),
            P(),
            P("fsdp", "tensor"),
            P("fsdp", "tensor"),
            P("fsdp", "tensor"),
            P("fsdp", "tensor"),
            P("tensor", None),
            P(("fsdp", "tensor"), None),
        ),
        out_specs=(
            P(("fsdp", "tensor"), None),
            P("fsdp", "tensor"),
            P("fsdp", "tensor"),
            P("fsdp", "tensor"),
            P("fsdp", "tensor"),
        ),
        check_vma=False,
    )
```

```python
import functools

import jax
import jax.numpy as jnp
import numpy as np
from jax import lax
from jax.experimental import pallas as pl
from jax.experimental.pallas import tpu as pltpu
from jax.sharding import PartitionSpec as P

BUCKETS = 32
MAX_DIST = 128
LEN = 256
EPSILON = 1e-06
MESH = pl.DeviceIdType.MESH
BF = jnp.bfloat16
F32 = jnp.float32
OUT, VAL, QRY, KEY = 0, 1, 2, 3


def bucket_steps():
    half_count = BUCKETS // 2
    exact_count = half_count // 2
    distance = np.arange(LEN)
    log_ratio = np.log(np.maximum(distance, 1) / exact_count) / np.log(MAX_DIST / exact_count)
    far = np.minimum(
        exact_count + np.floor(log_ratio * (half_count - exact_count)).astype(np.int64),
        half_count - 1,
    )
    bucket = np.where(distance < exact_count, distance, far)
    return [int(np.argmax(bucket >= k)) for k in range(half_count)]


def dot_nn(a, b):
    return lax.dot_general(a, b, (((1,), (0,)), ((), ())), preferred_element_type=F32)


def dot_nt(a, b):
    return lax.dot_general(a, b, (((1,), (1,)), ((), ())), preferred_element_type=F32)


class Links:
    def __init__(self, send_sem, recv_sem):
        self.send_sem, self.recv_sem = send_sem, recv_sem
        self.copies = {}

    def start(self, key, src, dst, peer):
        k = len(self.copies)
        copy = pltpu.make_async_remote_copy(
            src_ref=src,
            dst_ref=dst,
            send_sem=self.send_sem.at[k],
            recv_sem=self.recv_sem.at[k],
            device_id=peer,
            device_id_type=MESH,
        )
        copy.start()
        assert key not in self.copies
        self.copies[key] = copy

    def arrived(self, *key):
        self.copies[key].wait_recv()

    def finish(self):
        for copy in self.copies.values():
            copy.wait_send()


N_COPIES = 112


def kernel(
    x_ref, gain_ref, wq_ref, wk_ref, wv_ref, wo_ref, rb_ref, do_ref,
    dx_ref, gq_ref, gk_ref, gv_ref, go_ref,
    tok, cot, wgt, rel, bias, heads, dheads, rows_t,
    part_y, part_z, far_y, far_z, near_y, near_z, last,
    dn, dn_sib, far_x, near_x, splat, send_sem, recv_sem,
):
    f, t = lax.axis_index("fsdp"), lax.axis_index("tensor")
    x, zh, c = t // 4, (t // 2) % 2, t % 2
    y, zl = f // 2, f % 2
    z = zh * 2 + zl

    def dev(x, y, z, c):
        return (y * 2 + z % 2, (x * 2 + z // 2) * 2 + c)

    def xp(k):
        return (x + k) % 4

    def yp(k):
        return (y + k) % 4

    def zp(k):
        return (z + k) % 4

    sib = dev(x, y, z, 1 - c)
    to_x = {k: dev(xp(k), y, z, c) for k in (1, 3)}
    to_y = {k: dev(x, yp(k), z, c) for k in (1, 2, 3)}
    to_z = {k: dev(x, y, zp(k), c) for k in (1, 2, 3)}
    peers = [sib] + list(to_x.values()) + list(to_y.values()) + list(to_z.values())
    barrier = pltpu.get_barrier_semaphore()
    for peer in peers:
        pl.semaphore_signal(barrier, inc=1, device_id=peer, device_id_type=MESH)

    for w, ref in ((OUT, wo_ref), (VAL, wv_ref), (QRY, wq_ref), (KEY, wk_ref)):
        for u in range(2):
            wgt[u, w, z, y] = ref[:, u * 128 : u * 128 + 128]
    rel[zh] = jnp.zeros((8, 128), F32)
    rel[zh, 0:4, 0:32] = rb_ref[...]
    cot[x, c] = do_ref[...]

    net = Links(send_sem, recv_sem)

    def chunk(u, zz, yy, row, n):
        return wgt.at[u, pl.ds(0, 4), zz, yy, pl.ds(row, n)]

    def column(u, zz, row, n):
        return wgt.at[u, pl.ds(0, 4), zz, pl.ds(0, 4), pl.ds(row, n)]

    def line(u, yy, row, n):
        return wgt.at[u, pl.ds(0, 4), pl.ds(0, 4), yy, pl.ds(row, n)]

    def both_ways(name, src, to):
        net.start((name, 1), src, src, to[1])
        net.start((name, 3), src, src, to[3])

    def weights_a(u, hops):
        for k in hops:
            s = chunk(u, z, y, 0, 128)
            net.start(("y", u, k), s, s, to_y[k])
            s = chunk(u, z, y, 128, 128)
            net.start(("z", u, k), s, s, to_z[k])

    def weights_c(u):
        for k in (1, 3, 2):
            net.arrived("y", u, k)
        both_ways(("z2", u), column(u, z, 0, 128), to_z)
        for k in (1, 3, 2):
            net.arrived("z", u, k)
        both_ways(("y2", u), line(u, y, 128, 128), to_y)

    def weights_d(u):
        for k, row in ((1, 0), (3, 64)):
            net.arrived(("z2", u), k)
            s = column(u, zp(4 - k), row, 64)
            net.start(("z2f", u, k), s, s, to_z[k])
            net.arrived(("y2", u), k)
            s = line(u, yp(4 - k), 128 + row, 64)
            net.start(("y2f", u, k), s, s, to_y[k])

    def weights_here(u):
        for name in ("z2f", "y2f"):
            net.arrived(name, u, 1)
            net.arrived(name, u, 3)

    def tokens_a(name, buf):
        both_ways(name, buf.at[x, c], to_x)
        net.start((name, "sib", 0), buf.at[x, c], buf.at[x, c], sib)

    def tokens_b(name, buf):
        for k, row in ((1, 0), (3, 64)):
            net.arrived(name, k)
            s = buf.at[xp(4 - k), c, pl.ds(row, 64)]
            net.start((name, "f", k), s, s, to_x[k])
            s = buf.at[xp(4 - k), c]
            net.start((name, "sib", 4 - k), s, s, sib)

    def tokens_c(name, buf):
        net.arrived(name, "f", 1)
        net.arrived(name, "f", 3)
        s = buf.at[xp(2), c]
        net.start((name, "sib", 2), s, s, sib)

    def norm_rows(k):
        rows = x_ref[pl.ds(pl.multiple_of(k * 16, 16), 16), :].astype(F32)
        inv = lax.rsqrt(jnp.mean(rows * rows, axis=-1, keepdims=True) + EPSILON)
        return rows * inv, inv

    def normalize():
        @pl.loop(0, 8)
        def _(k):
            unit, _ = norm_rows(k)
            tok[x, c, pl.ds(pl.multiple_of(k * 16, 16), 16), :] = (unit * gain_ref[...]).astype(BF)

    def spread_bias():
        net.arrived("rel")
        steps = bucket_steps()
        table = jnp.concatenate([rel[0, 0:4, :], rel[1, 0:4, :]], axis=0)
        for k in range(BUCKETS):
            splat[k] = jnp.broadcast_to(table[:, k : k + 1], (8, 128))

        @pl.loop(0, LEN // 8)
        def _(k):
            i = lax.broadcasted_iota(jnp.int32, (8, LEN), 0) + k * 8
            r = lax.broadcasted_iota(jnp.int32, (8, LEN), 1) - i

            def row(b, h):
                return jnp.broadcast_to(splat[b, h : h + 1, 0:1], (8, LEN))

            values = [row(0, h) for h in range(8)]
            for b in range(1, BUCKETS // 2):
                for chosen, at in ((r <= -steps[b], b), (r >= steps[b], BUCKETS // 2 + b)):
                    for h in range(8):
                        values[h] = jnp.where(chosen, row(at, h), values[h])
            for h in range(8):
                bias[h, pl.ds(pl.multiple_of(k * 8, 8), 8), :] = values[h]

    lane = lax.broadcasted_iota(jnp.int32, (1, 128), 1)
    mask = [(lane < 64).astype(F32).astype(BF), (lane >= 64).astype(F32).astype(BF)]
    row_at = lax.broadcasted_iota(jnp.int32, (128, 1), 0)
    mask_t = [(row_at < 64).astype(F32).astype(BF), (row_at >= 64).astype(F32).astype(BF)]

    def passages(u, places):
        n = len(places)

        def by_chunk(buf):
            whole = jnp.concatenate([buf[p].reshape(256, 2048) for p in places], axis=0)
            order = [yy * 2 + zz for zz in range(2) for yy in range(4)]
            return jnp.concatenate([whole[:, i * 256 : i * 256 + 256] for i in order], axis=1)

        for w in range(4):
            left = by_chunk(cot if w == OUT else tok)
            right = jnp.concatenate([wgt[u, w, g * 2 : g * 2 + 2].reshape(2048, 128) for g in range(2)], axis=1)
            heads[w, 0 : n * 256] = dot_nn(left, right).astype(BF)
        for i, p in enumerate(places):
            attention(u, i, pl.ds(pl.multiple_of(p * 256, 256), 256))

    def attention(u, i, rows):
        parts = [
            tuple(heads[w, i * 256 : i * 256 + 256, g * 128 : g * 128 + 128] for w in range(4)) for g in range(2)
        ]
        scores = [
            [dot_nt(q2 * mask[h], k2) + bias[g * 4 + u * 2 + h] for h in range(2)]
            for g, (_, _, q2, k2) in enumerate(parts)
        ]
        d_prob = [[dot_nt(dc2 * mask[h], v2) for h in range(2)] for dc2, v2, _, _ in parts]
        probs_b, d_score = [[], []], [[], []]
        for g in range(2):
            for h in range(2):
                e = jnp.exp(scores[g][h] - jnp.max(scores[g][h], axis=-1, keepdims=True))
                probs = e * (1.0 / jnp.sum(e, axis=-1, keepdims=True))
                row_dot = jnp.sum(probs * d_prob[g][h], axis=-1, keepdims=True)
                probs_b[g].append(probs.astype(BF))
                d_score[g].append((probs * (d_prob[g][h] - row_dot)).astype(BF))
        for g, (dc2, v2, q2, k2) in enumerate(parts):
            ctx = dot_nn(
                jnp.concatenate(probs_b[g], axis=1),
                jnp.concatenate([v2 * mask[0], v2 * mask[1]], axis=0),
            ).astype(BF)
            dq = dot_nn(
                jnp.concatenate(d_score[g], axis=1),
                jnp.concatenate([k2 * mask[0], k2 * mask[1]], axis=0),
            ).astype(BF)
            dc_t, q_t = dc2.T, q2.T
            dv_t = dot_nn(
                jnp.concatenate([dc_t * mask_t[0], dc_t * mask_t[1]], axis=1),
                jnp.concatenate(probs_b[g], axis=0),
            ).astype(BF)
            dk_t = dot_nn(
                jnp.concatenate([q_t * mask_t[0], q_t * mask_t[1]], axis=1),
                jnp.concatenate(d_score[g], axis=0),
            ).astype(BF)
            at, lanes = pl.ds(g * 128, 128), pl.ds(g * 128, 128)
            rows_t[OUT, at, rows] = ctx.T
            rows_t[VAL, at, rows] = dv_t
            rows_t[QRY, at, rows] = dq.T
            rows_t[KEY, at, rows] = dk_t
            dheads[u, VAL - 1, rows, lanes] = dv_t.T
            dheads[u, QRY - 1, rows, lanes] = dq
            dheads[u, KEY - 1, rows, lanes] = dk_t.T

    def weight_grads(u, pair):
        if pair == 0:
            out = dot_nn(rows_t[OUT], cot[...].reshape(1024, 2048)).astype(BF)
            val = dot_nn(rows_t[VAL], tok[...].reshape(1024, 2048)).astype(BF)
            res = (out, val)
        else:
            both = dot_nn(rows_t[2:4].reshape(512, 1024), tok[...].reshape(1024, 2048)).astype(BF)
            res = (both[:256], both[256:])
        for w in range(2):
            for f in range(8):
                fy, fz = f // 2, f % 2
                for g in range(2):
                    for h in range(2):
                        at = g * 128 + h * 64
                        block = res[w][at : at + 64, f * 256 : f * 256 + 256]
                        if pair == 0:
                            part_y[u, fy, h, w, g, fz] = block
                        else:
                            part_z[u, g * 2 + fz, h, w, fy] = block

    def ring_far(key, block, far, near, to):
        net.start((key, "far", 1), block(2, 0), far(0), to[1])
        net.start((key, "far", 3), block(2, 1), far(1), to[3])

    def ring_near(k, key, block, far, near, to):
        half, side = (1, 0) if k == 1 else (0, 1)
        net.start((key, "near", k), block(k, half), near(side, half), to[k])

    def ring_both(k, add, key, block, far, near, to):
        half, side = (0, 0) if k == 1 else (1, 1)
        net.arrived(key, "far", k)
        add(block(k, half), far(side))
        net.start((key, "both", k), block(k, half), near(side, half), to[k])

    def ring_c(key):
        for k in (1, 3):
            net.arrived(key, "near", k)
            net.arrived(key, "both", k)

    def add_into(dst, src):
        dst[...] = (dst[...].astype(F32) + src[...].astype(F32)).astype(BF)

    def add_pair(dst, src):
        for w in range(2):
            add_into(dst.at[w], src.at[w])

    def first(u, pair):
        if pair == 0:
            return (
                ("s1", u, pair),
                lambda k, h: part_y.at[u, yp(k), h],
                lambda s: far_y.at[u, s],
                lambda s, h: near_y.at[u, s, h],
                to_y,
            )
        return (
            ("s1", u, pair),
            lambda k, h: part_z.at[u, zp(k), h],
            lambda s: far_z.at[u, s],
            lambda s, h: near_z.at[u, s, h],
            to_z,
        )

    def grads_a(u, pair):
        ring_far(*first(u, pair))
        for k in (1, 3):
            ring_near(k, *first(u, pair))

    def grads_b(u):
        for k in (1, 3):
            for pair in range(2):
                ring_both(k, add_pair, *first(u, pair))

    def grads_c(u):
        for pair in range(2):
            ring_c(first(u, pair)[0])
            own, near = (part_y.at[u, y], near_y.at[u]) if pair == 0 else (part_z.at[u, z], near_z.at[u])
            for h in range(2):
                for w in range(2):
                    total = own[h, w].astype(F32) + near[0, h, w].astype(F32) + near[1, h, w].astype(F32)
                    own[h, w] = total.astype(BF)
            for k in (2, 1, 3):
                if pair == 0:
                    src, to = part_y.at[u, y, pl.ds(0, 2), pl.ds(0, 2), zp(k) // 2, zp(k) % 2], to_z[k]
                else:
                    src, to = part_z.at[u, z, pl.ds(0, 2), pl.ds(0, 2), yp(k)], to_y[k]
                net.start(("s2", u, pair, k), src, last.at[u, pair, k - 1], to)

    def grads_e(u):
        for pair, outs in ((0, (go_ref, gv_ref)), (1, (gq_ref, gk_ref))):
            for k in (1, 3, 2):
                net.arrived("s2", u, pair, k)
            for w in range(2):
                for h in range(2):
                    own = part_y[u, y, h, w, zh, zl] if pair == 0 else part_z[u, z, h, w, y]
                    total = own.astype(F32)
                    for k in range(3):
                        total = total + last[u, pair, k, h, w].astype(F32)
                    outs[w][:, u * 128 + h * 64 : u * 128 + h * 64 + 64] = total.T

    def d_tokens(first, second):
        places = (xp(first), xp(second))
        pieces = [(u, w, g) for u in range(2) for w in range(3) for g in range(2)]
        left = jnp.concatenate(
            [
                jnp.concatenate(
                    [
                        dheads[u, w, pl.ds(pl.multiple_of(p * 256, 256), 256), g * 128 : g * 128 + 128]
                        for u, w, g in pieces
                    ],
                    axis=1,
                )
                for p in places
            ],
            axis=0,
        )
        for f in range(8):
            right = jnp.concatenate([wgt[u, w + 1, g * 2 + f % 2, f // 2] for u, w, g in pieces], axis=1)
            total = dot_nt(left, right).astype(BF)
            for i, p in enumerate(places):
                dn[p, :, :, f * 256 : f * 256 + 256] = total[i * 256 : i * 256 + 256].reshape(2, 128, 256)

    def d_cross(k):
        net.start(("dsib", k), dn.at[xp(k), 1 - c], dn_sib.at[xp(k)], sib)

    def add_rows(dst, src, n):
        @pl.loop(0, n // 16)
        def _(m):
            rows = pl.ds(pl.multiple_of(m * 16, 16), 16)
            dst[rows, :] = (dst[rows, :].astype(F32) + src[rows, :].astype(F32)).astype(BF)

    def d_merge(k):
        net.arrived("dsib", k)
        add_rows(dn.at[xp(k), c], dn_sib.at[xp(k)], 128)

    d_ring = (
        "dx",
        lambda k, h: dn.at[xp(k), c, pl.ds(h * 64, 64)],
        lambda s: far_x.at[s],
        lambda s, h: near_x.at[s, pl.ds(h * 64, 64)],
        to_x,
    )

    def d_inputs():
        ring_c(d_ring[0])

        @pl.loop(0, 8)
        def _(m):
            rows = pl.ds(pl.multiple_of(m * 16, 16), 16)
            unit, inv = norm_rows(m)
            d_normed = dn[x, c, rows, :].astype(F32) + near_x[0, rows, :].astype(F32) + near_x[1, rows, :].astype(F32)
            d_unit = d_normed * gain_ref[...]
            branch = inv * (d_unit - unit * jnp.mean(d_unit * unit, axis=-1, keepdims=True))
            dx_ref[rows, :] = (do_ref[rows, :].astype(F32) + branch).astype(BF)

    def d_add(dst, src):
        add_rows(dst, src, 64)

    normalize()
    pl.semaphore_wait(barrier, len(peers))
    weights_a(0, (2, 1, 3))
    tokens_a("cot", cot)
    tokens_a("tok", tok)
    net.start(("rel",), rel.at[zh], rel.at[zh], to_z[2])
    weights_a(1, (2,))
    weights_c(0)
    spread_bias()
    weights_a(1, (1, 3))
    tokens_b("cot", cot)
    weights_d(0)
    tokens_b("tok", tok)
    weights_here(0)
    weights_c(1)
    net.arrived("cot", "sib", 0)
    net.arrived("tok", "sib", 0)
    passages(0, [x])
    for name in ("cot", "tok"):
        net.arrived(name, "sib", 1)
        net.arrived(name, "sib", 3)
    tokens_c("cot", cot)
    passages(0, [xp(1), xp(3)])
    tokens_c("tok", tok)
    net.arrived("cot", "sib", 2)
    net.arrived("tok", "sib", 2)
    passages(0, [xp(2)])
    weight_grads(0, 0)
    weights_d(1)
    grads_a(0, 0)
    weight_grads(0, 1)
    grads_a(0, 1)
    weights_here(1)
    passages(1, [0, 1])
    grads_b(0)
    passages(1, [2, 3])
    weight_grads(1, 0)
    grads_a(1, 0)
    weight_grads(1, 1)
    grads_a(1, 1)
    grads_c(0)
    d_tokens(2, 1)
    d_cross(2)
    d_cross(1)
    d_merge(2)
    ring_far(*d_ring)
    d_merge(1)
    ring_near(1, *d_ring)
    grads_b(1)
    d_tokens(3, 0)
    d_cross(3)
    d_cross(0)
    ring_both(1, d_add, *d_ring)
    d_merge(3)
    ring_near(3, *d_ring)
    ring_both(3, d_add, *d_ring)
    grads_e(0)
    d_merge(0)
    grads_c(1)
    d_inputs()
    grads_e(1)
    net.finish()


def write_results(*refs):
    n = len(refs) // 2
    for src, dst in zip(refs[:n], refs[n:]):
        dst[...] = src[...]


def per_device(inputs, gain, w_query, w_key, w_value, w_out, rel_bias, d_output):
    vmem = pl.BlockSpec(memory_space=pltpu.VMEM)
    grad = jax.ShapeDtypeStruct((256, 256), F32)
    shapes = (jax.ShapeDtypeStruct((128, 2048), BF), grad, grad, grad, grad)
    results = pl.pallas_call(
        kernel,
        out_shape=shapes,
        in_specs=[vmem] * 8,
        out_specs=(vmem,) * 5,
        scratch_shapes=[
            pltpu.VMEM((4, 2, 128, 2048), BF),
            pltpu.VMEM((4, 2, 128, 2048), BF),
            pltpu.VMEM((2, 4, 4, 4, 256, 128), BF),
            pltpu.VMEM((2, 8, 128), F32),
            pltpu.VMEM((8, 256, 256), F32),
            pltpu.VMEM((4, 1024, 256), BF),
            pltpu.VMEM((2, 3, 1024, 256), BF),
            pltpu.VMEM((4, 256, 1024), BF),
            pltpu.VMEM((2, 4, 2, 2, 2, 2, 64, 256), BF),
            pltpu.VMEM((2, 4, 2, 2, 4, 64, 256), BF),
            pltpu.VMEM((2, 2, 2, 2, 2, 64, 256), BF),
            pltpu.VMEM((2, 2, 2, 4, 64, 256), BF),
            pltpu.VMEM((2, 2, 2, 2, 2, 2, 64, 256), BF),
            pltpu.VMEM((2, 2, 2, 2, 4, 64, 256), BF),
            pltpu.VMEM((2, 2, 3, 2, 2, 64, 256), BF),
            pltpu.VMEM((4, 2, 128, 2048), BF),
            pltpu.VMEM((4, 128, 2048), BF),
            pltpu.VMEM((2, 64, 2048), BF),
            pltpu.VMEM((2, 128, 2048), BF),
            pltpu.VMEM((32, 8, 128), F32),
            pltpu.SemaphoreType.DMA((N_COPIES,)),
            pltpu.SemaphoreType.DMA((N_COPIES,)),
        ],
        compiler_params=pltpu.CompilerParams(
            collective_id=0, has_side_effects=True, vmem_limit_bytes=62 * 1024 * 1024
        ),
        name="attention_backward",
    )(inputs, gain.reshape(1, -1), w_query, w_key, w_value, w_out, rel_bias, d_output)
    return pl.pallas_call(
        write_results,
        out_shape=shapes,
        in_specs=[vmem] * 5,
        out_specs=(vmem,) * 5,
        name="write_results",
    )(*results)


def solution(mesh):
    return jax.shard_map(
        per_device,
        mesh=mesh,
        in_specs=(
            P(("fsdp", "tensor"), None),
            P(),
            P("fsdp", "tensor"),
            P("fsdp", "tensor"),
            P("fsdp", "tensor"),
            P("fsdp", "tensor"),
            P("tensor", None),
            P(("fsdp", "tensor"), None),
        ),
        out_specs=(
            P(("fsdp", "tensor"), None),
            P("fsdp", "tensor"),
            P("fsdp", "tensor"),
            P("fsdp", "tensor"),
            P("fsdp", "tensor"),
        ),
        check_vma=False,
    )
```

```python
import functools

import jax
import jax.numpy as jnp
import numpy as np
from jax import lax
from jax.experimental import pallas as pl
from jax.experimental.pallas import tpu as pltpu
from jax.sharding import PartitionSpec as P

BUCKETS = 32
MAX_DIST = 128
LEN = 256
EPSILON = 1e-06
MESH = pl.DeviceIdType.MESH
BF = jnp.bfloat16
F32 = jnp.float32
OUT, VAL, QRY, KEY = 0, 1, 2, 3


def bucket_steps():
    half_count = BUCKETS // 2
    exact_count = half_count // 2
    distance = np.arange(LEN)
    log_ratio = np.log(np.maximum(distance, 1) / exact_count) / np.log(MAX_DIST / exact_count)
    far = np.minimum(
        exact_count + np.floor(log_ratio * (half_count - exact_count)).astype(np.int64),
        half_count - 1,
    )
    bucket = np.where(distance < exact_count, distance, far)
    return [int(np.argmax(bucket >= k)) for k in range(half_count)]


def dot_nn(a, b):
    return lax.dot_general(a, b, (((1,), (0,)), ((), ())), preferred_element_type=F32)


def dot_nt(a, b):
    return lax.dot_general(a, b, (((1,), (1,)), ((), ())), preferred_element_type=F32)


class Links:
    def __init__(self, send_sem, recv_sem):
        self.send_sem, self.recv_sem = send_sem, recv_sem
        self.groups = {}
        self.sends = {}

    def start(self, group, send, src, dst, peer):
        k = self.groups.setdefault(group, len(self.groups))
        j = self.sends.setdefault(send, len(self.sends))
        pltpu.make_async_remote_copy(
            src_ref=src,
            dst_ref=dst,
            send_sem=self.send_sem.at[j],
            recv_sem=self.recv_sem.at[k],
            device_id=peer,
            device_id_type=MESH,
        ).start()

    def waiter(self, j, k, ref, peer):
        return pltpu.make_async_remote_copy(
            src_ref=ref,
            dst_ref=ref,
            send_sem=self.send_sem.at[j],
            recv_sem=self.recv_sem.at[k],
            device_id=peer,
            device_id_type=MESH,
        )

    def arrived(self, group, ref, peer):
        self.waiter(0, self.groups[group], ref, peer).wait_recv()

    def sent(self, send, ref, peer):
        self.waiter(self.sends[send], 0, ref, peer).wait_send()


N_GROUPS, N_SENDS = 63, 6


def kernel(
    x_in, gain_in, wq_in, wk_in, wv_in, wo_in, rb_in, do_in,
    dx_ref, gq_ref, gk_ref, gv_ref, go_ref,
    tok, cot, wgt, rel, bias, heads, dheads, rows_t,
    part_y, part_z, far_y, far_z, near_y, near_z, far2, near2,
    dn, dn_sib, far_x, near_x, splat, x_ref, gain_ref, rb_ref, send_sem, recv_sem, load_sem,
):
    f, t = lax.axis_index("fsdp"), lax.axis_index("tensor")
    x, zh, c = t // 4, (t // 2) % 2, t % 2
    y, zl = f // 2, f % 2
    z = zh * 2 + zl

    def dev(x, y, z, c):
        return (y * 2 + z % 2, (x * 2 + z // 2) * 2 + c)

    def xp(k):
        return (x + k) % 4

    def yp(k):
        return (y + k) % 4

    def zp(k):
        return (z + k) % 4

    sib = dev(x, y, z, 1 - c)
    to_x = {k: dev(xp(k), y, z, c) for k in (1, 3)}
    to_y = {k: dev(x, yp(k), z, c) for k in (1, 2, 3)}
    to_z = {k: dev(x, y, zp(k), c) for k in (1, 2, 3)}
    peers = [sib] + list(to_x.values()) + list(to_y.values()) + list(to_z.values())
    barrier = pltpu.get_barrier_semaphore()
    for peer in peers:
        pl.semaphore_signal(barrier, inc=1, device_id=peer, device_id_type=MESH)

    loads = [(x_in, x_ref, 0), (gain_in, gain_ref, 1), (rb_in, rb_ref, 2), (do_in, cot.at[x, c], 3)]
    for u in range(2):
        for w, ref in ((OUT, wo_in), (VAL, wv_in), (QRY, wq_in), (KEY, wk_in)):
            loads.append((ref.at[:, pl.ds(u * 128, 128)], wgt.at[u, w, z, y], 4))
    for src, dst, i in loads:
        pltpu.make_async_copy(src, dst, load_sem.at[i]).start()

    def loaded(i, ref):
        pltpu.make_async_copy(ref, ref, load_sem.at[i]).wait()

    net = Links(send_sem, recv_sem)

    def chunk(u, zz, yy, row, n):
        return wgt.at[u, pl.ds(0, 4), zz, yy, pl.ds(row, n)]

    def column(u, zz, row, n):
        return wgt.at[u, pl.ds(0, 4), zz, pl.ds(0, 4), pl.ds(row, n)]

    def line(u, yy, row, n):
        return wgt.at[u, pl.ds(0, 4), pl.ds(0, 4), yy, pl.ds(row, n)]

    def arrived(group, ref):
        net.arrived(group, ref, sib)

    def weights_a(u):
        for part in range(2):
            for k, row in ((1, part * 64), (3, 64 - part * 64)):
                for name, to, at in (("y", to_y, 0), ("z", to_z, 128)):
                    s = chunk(u, z, y, at + row, 64)
                    net.start((name, u) if part else (name, u, k), "w", s, s, to[k])

    def weights_b(u):
        for k, row in ((1, 0), (3, 64)):
            s = chunk(u, z, yp(4 - k), row, 64)
            arrived(("y", u, k), s)
            net.start(("y", u), "w", s, s, to_y[k])
            s = chunk(u, zp(4 - k), y, 128 + row, 64)
            arrived(("z", u, k), s)
            net.start(("z", u), "w", s, s, to_z[k])

    def weights_c(u):
        arrived(("y", u), column(u, z, 0, 64))
        for part in range(2):
            for k, row in ((1, part * 64), (3, 64 - part * 64)):
                s = column(u, z, row, 64)
                net.start(("all", u) if part else ("z2", u, k), "w", s, s, to_z[k])
        arrived(("z", u), line(u, y, 128, 64))
        for part in range(2):
            for k, row in ((1, part * 64), (3, 64 - part * 64)):
                s = line(u, y, 128 + row, 64)
                net.start(("all", u) if part else ("y2", u, k), "w", s, s, to_y[k])

    def weights_d(u):
        for k, row in ((1, 0), (3, 64)):
            s = column(u, zp(4 - k), row, 64)
            arrived(("z2", u, k), s)
            net.start(("all", u), "w", s, s, to_z[k])
            s = line(u, yp(4 - k), 128 + row, 64)
            arrived(("y2", u, k), s)
            net.start(("all", u), "w", s, s, to_y[k])

    def weights_here(u):
        arrived(("all", u), wgt.at[u, pl.ds(0, 4), pl.ds(0, 4), pl.ds(0, 4), pl.ds(0, 128)])

    def tokens_a(name, buf):
        for k in (1, 3):
            net.start((name, k), name, buf.at[x, c], buf.at[x, c], to_x[k])
        net.start("own", name, buf.at[x, c], buf.at[x, c], sib)

    def tokens_b(name, buf):
        for k, row in ((1, 0), (3, 64)):
            arrived((name, k), buf.at[xp(4 - k), c])
            s = buf.at[xp(4 - k), c, pl.ds(row, 64)]
            net.start((name, "far"), name, s, s, to_x[k])
            s = buf.at[xp(4 - k), c]
            net.start("near", name, s, s, sib)

    def tokens_c(name, buf):
        s = buf.at[xp(2), c]
        arrived((name, "far"), s)
        net.start("far", name, s, s, sib)

    def norm_rows(k):
        rows = x_ref[pl.ds(pl.multiple_of(k * 16, 16), 16), :].astype(F32)
        inv = lax.rsqrt(jnp.mean(rows * rows, axis=-1, keepdims=True) + EPSILON)
        return rows * inv, inv

    def normalize():
        @pl.loop(0, 8)
        def _(k):
            unit, _ = norm_rows(k)
            tok[x, c, pl.ds(pl.multiple_of(k * 16, 16), 16), :] = (unit * gain_ref[...]).astype(BF)

    def spread_bias():
        arrived("rel", rel.at[zh])
        steps = bucket_steps()
        table = jnp.concatenate([rel[0, 0:4, :], rel[1, 0:4, :]], axis=0)
        for k in range(BUCKETS):
            splat[k] = jnp.broadcast_to(table[:, k : k + 1], (8, 128))

        @pl.loop(0, LEN // 8)
        def _(k):
            i = lax.broadcasted_iota(jnp.int32, (8, LEN), 0) + k * 8
            r = lax.broadcasted_iota(jnp.int32, (8, LEN), 1) - i

            def row(b, h):
                return jnp.broadcast_to(splat[b, h : h + 1, 0:1], (8, LEN))

            values = [row(0, h) for h in range(8)]
            for b in range(1, BUCKETS // 2):
                for chosen, at in ((r <= -steps[b], b), (r >= steps[b], BUCKETS // 2 + b)):
                    for h in range(8):
                        values[h] = jnp.where(chosen, row(at, h), values[h])
            for h in range(8):
                bias[h, pl.ds(pl.multiple_of(k * 8, 8), 8), :] = values[h]

    lane = lax.broadcasted_iota(jnp.int32, (1, 128), 1)
    mask = [(lane < 64).astype(F32).astype(BF), (lane >= 64).astype(F32).astype(BF)]
    row_at = lax.broadcasted_iota(jnp.int32, (128, 1), 0)
    mask_t = [(row_at < 64).astype(F32).astype(BF), (row_at >= 64).astype(F32).astype(BF)]

    def passages(u, places):
        n = len(places)

        def by_chunk(buf):
            whole = jnp.concatenate([buf[p].reshape(256, 2048) for p in places], axis=0)
            order = [yy * 2 + zz for zz in range(2) for yy in range(4)]
            return jnp.concatenate([whole[:, i * 256 : i * 256 + 256] for i in order], axis=1)

        for w in range(4):
            left = by_chunk(cot if w == OUT else tok)
            right = jnp.concatenate([wgt[u, w, g * 2 : g * 2 + 2].reshape(2048, 128) for g in range(2)], axis=1)
            heads[w, 0 : n * 256] = dot_nn(left, right).astype(BF)
        for i, p in enumerate(places):
            attention(u, i, pl.ds(pl.multiple_of(p * 256, 256), 256))

    def attention(u, i, rows):
        parts = [
            tuple(heads[w, i * 256 : i * 256 + 256, g * 128 : g * 128 + 128] for w in range(4)) for g in range(2)
        ]
        scores = [
            [dot_nt(q2 * mask[h], k2) + bias[g * 4 + u * 2 + h] for h in range(2)]
            for g, (_, _, q2, k2) in enumerate(parts)
        ]
        d_prob = [[dot_nt(dc2 * mask[h], v2) for h in range(2)] for dc2, v2, _, _ in parts]
        probs_b, d_score = [[], []], [[], []]
        for g in range(2):
            for h in range(2):
                e = jnp.exp(scores[g][h] - jnp.max(scores[g][h], axis=-1, keepdims=True))
                probs = e * (1.0 / jnp.sum(e, axis=-1, keepdims=True))
                row_dot = jnp.sum(probs * d_prob[g][h], axis=-1, keepdims=True)
                probs_b[g].append(probs.astype(BF))
                d_score[g].append((probs * (d_prob[g][h] - row_dot)).astype(BF))
        for g, (dc2, v2, q2, k2) in enumerate(parts):
            ctx = dot_nn(
                jnp.concatenate(probs_b[g], axis=1),
                jnp.concatenate([v2 * mask[0], v2 * mask[1]], axis=0),
            ).astype(BF)
            dq = dot_nn(
                jnp.concatenate(d_score[g], axis=1),
                jnp.concatenate([k2 * mask[0], k2 * mask[1]], axis=0),
            ).astype(BF)
            dc_t, q_t = dc2.T, q2.T
            dv_t = dot_nn(
                jnp.concatenate([dc_t * mask_t[0], dc_t * mask_t[1]], axis=1),
                jnp.concatenate(probs_b[g], axis=0),
            ).astype(BF)
            dk_t = dot_nn(
                jnp.concatenate([q_t * mask_t[0], q_t * mask_t[1]], axis=1),
                jnp.concatenate(d_score[g], axis=0),
            ).astype(BF)
            at, lanes = pl.ds(g * 128, 128), pl.ds(g * 128, 128)
            rows_t[OUT, at, rows] = ctx.T
            rows_t[VAL, at, rows] = dv_t
            rows_t[QRY, at, rows] = dq.T
            rows_t[KEY, at, rows] = dk_t
            dheads[u, VAL - 1, rows, lanes] = dv_t.T
            dheads[u, QRY - 1, rows, lanes] = dq
            dheads[u, KEY - 1, rows, lanes] = dk_t.T

    def weight_grads(u, pair):
        if pair == 0:
            out = dot_nn(rows_t[OUT], cot[...].reshape(1024, 2048)).astype(BF)
            val = dot_nn(rows_t[VAL], tok[...].reshape(1024, 2048)).astype(BF)
            res = (out, val)
        else:
            both = dot_nn(rows_t[2:4].reshape(512, 1024), tok[...].reshape(1024, 2048)).astype(BF)
            res = (both[:256], both[256:])
        for w in range(2):
            for f in range(8):
                fy, fz = f // 2, f % 2
                for g in range(2):
                    for h in range(2):
                        at = g * 128 + h * 64
                        block = res[w][at : at + 64, f * 256 : f * 256 + 256]
                        if pair == 0:
                            part_y[u, fy, h, w, g, fz] = block
                        else:
                            part_z[u, g * 2 + fz, h, w, fy] = block

    def ring_far(key, block, far, near, to, send):
        net.start((key, 1), send, block(2, 0), far(0), to[1])
        net.start((key, 3), send, block(2, 1), far(1), to[3])

    def ring_near(k, key, block, far, near, to, send):
        half, side = (1, 0) if k == 1 else (0, 1)
        net.start(key, send, block(k, half), near(side, half), to[k])

    def ring_both(k, add, key, block, far, near, to, send):
        half, side = (0, 0) if k == 1 else (1, 1)
        arrived((key, k), far(side))
        add(block(k, half), far(side))
        net.start(key, send, block(k, half), near(side, half), to[k])

    def add_into(dst, src):
        dst[...] = (dst[...].astype(F32) + src[...].astype(F32)).astype(BF)

    def add_pair(dst, src):
        for w in range(2):
            add_into(dst.at[w], src.at[w])

    def first(u, pair):
        if pair == 0:
            return (
                ("s1", u, pair),
                lambda k, h: part_y.at[u, yp(k), h],
                lambda s: far_y.at[u, s],
                lambda s, h: near_y.at[u, s, h],
                to_y,
                "sums",
            )
        return (
            ("s1", u, pair),
            lambda k, h: part_z.at[u, zp(k), h],
            lambda s: far_z.at[u, s],
            lambda s, h: near_z.at[u, s, h],
            to_z,
            "sums",
        )

    def second(u, pair):
        def block(k, h):
            if pair == 0:
                return part_y.at[u, y, h, pl.ds(0, 2), zp(k) // 2, zp(k) % 2]
            return part_z.at[u, z, h, pl.ds(0, 2), yp(k)]

        return (
            ("s2", u, pair),
            block,
            lambda s: far2.at[u, pair, s],
            lambda s, h: near2.at[u, pair, s, h],
            to_z if pair == 0 else to_y,
            "sums",
        )

    def grads_a(u, pair):
        ring_far(*first(u, pair))
        for k in (1, 3):
            ring_near(k, *first(u, pair))

    def grads_b(u):
        for k in (1, 3):
            for pair in range(2):
                ring_both(k, add_pair, *first(u, pair))

    def grads_c(u):
        for pair in range(2):
            own, near = (part_y.at[u, y], near_y.at[u]) if pair == 0 else (part_z.at[u, z], near_z.at[u])
            arrived(("s1", u, pair), near)
            for h in range(2):
                for w in range(2):
                    total = own[h, w].astype(F32) + near[0, h, w].astype(F32) + near[1, h, w].astype(F32)
                    own[h, w] = total.astype(BF)
            ring_far(*second(u, pair))

    def grads_near(u):
        for pair in range(2):
            for k in (1, 3):
                ring_near(k, *second(u, pair))

    def grads_d(u):
        for k in (1, 3):
            for pair in range(2):
                ring_both(k, add_into, *second(u, pair))

    def grads_e(u):
        for pair, outs in ((0, (go_ref, gv_ref)), (1, (gq_ref, gk_ref))):
            near = near2.at[u, pair]
            arrived(("s2", u, pair), near)
            for w in range(2):
                for h in range(2):
                    own = part_y[u, y, h, w, zh, zl] if pair == 0 else part_z[u, z, h, w, y]
                    total = own.astype(F32) + near[0, h, w].astype(F32) + near[1, h, w].astype(F32)
                    outs[w][:, u * 128 + h * 64 : u * 128 + h * 64 + 64] = total.T

    def d_tokens(u, places):
        pieces = [(w, g) for w in range(3) for g in range(2)]
        left = jnp.concatenate(
            [
                jnp.concatenate([dheads[u, w, pl.ds(pl.multiple_of(p * 256, 256), 256), :] for w in range(3)], axis=1)
                for p in places
            ],
            axis=0,
        )
        for f in range(8):
            cols = pl.ds(f * 256, 256)
            right = jnp.concatenate([wgt[u, w + 1, g * 2 + f % 2, f // 2] for w, g in pieces], axis=1)
            total = dot_nt(left, right)
            for i, p in enumerate(places):
                block = total[i * 256 : i * 256 + 256].reshape(2, 128, 256)
                if u:
                    block = block + dn[p, :, :, cols].astype(F32)
                dn[p, :, :, cols] = block.astype(BF)

    def d_cross(k):
        net.start(("cross", k), "dn", dn.at[xp(k), 1 - c], dn_sib.at[xp(k)], sib)

    def add_rows(dst, src, n):
        @pl.loop(0, n // 16)
        def _(m):
            rows = pl.ds(pl.multiple_of(m * 16, 16), 16)
            dst[rows, :] = (dst[rows, :].astype(F32) + src[rows, :].astype(F32)).astype(BF)

    def d_merge(k):
        arrived(("cross", k), dn_sib.at[xp(k)])
        add_rows(dn.at[xp(k), c], dn_sib.at[xp(k)], 128)

    d_ring = (
        "dx",
        lambda k, h: dn.at[xp(k), c, pl.ds(h * 64, 64)],
        lambda s: far_x.at[s],
        lambda s, h: near_x.at[s, pl.ds(h * 64, 64)],
        to_x,
        "dn",
    )

    def d_inputs():
        arrived("dx", near_x)

        @pl.loop(0, 8)
        def _(m):
            rows = pl.ds(pl.multiple_of(m * 16, 16), 16)
            unit, inv = norm_rows(m)
            d_normed = dn[x, c, rows, :].astype(F32) + near_x[0, rows, :].astype(F32) + near_x[1, rows, :].astype(F32)
            d_unit = d_normed * gain_ref[...]
            branch = inv * (d_unit - unit * jnp.mean(d_unit * unit, axis=-1, keepdims=True))
            dx_ref[rows, :] = (cot[x, c, rows, :].astype(F32) + branch).astype(BF)

    def d_add(dst, src):
        add_rows(dst, src, 64)

    loaded(2, rb_ref)
    rel[zh] = jnp.zeros((8, 128), F32)
    rel[zh, 0:4, 0:32] = rb_ref[...]
    loaded(0, x_ref)
    loaded(1, gain_ref)
    normalize()
    loaded(3, cot.at[x, c])
    loaded(4, wgt.at[pl.ds(0, 2), pl.ds(0, 4), z, y])
    pl.semaphore_wait(barrier, len(peers))
    weights_a(0)
    tokens_a("cot", cot)
    tokens_a("tok", tok)
    net.start("rel", "rel", rel.at[zh], rel.at[zh], to_z[2])
    weights_b(0)
    weights_a(1)
    weights_c(0)
    weights_b(1)
    spread_bias()
    weights_d(0)
    tokens_b("cot", cot)
    weights_c(1)
    tokens_b("tok", tok)
    weights_here(0)
    arrived("own", tok.at[pl.ds(0, 2), 0])
    passages(0, [x])
    arrived("near", tok.at[pl.ds(0, 4), 0])
    tokens_c("cot", cot)
    passages(0, [xp(1), xp(3)])
    weights_d(1)
    tokens_c("tok", tok)
    arrived("far", tok.at[pl.ds(0, 2), 0])
    passages(0, [xp(2)])
    weight_grads(0, 0)
    grads_a(0, 0)
    weight_grads(0, 1)
    grads_a(0, 1)
    d_tokens(0, [0, 1, 2, 3])
    weights_here(1)
    passages(1, [0, 1])
    grads_b(0)
    passages(1, [2, 3])
    weight_grads(1, 0)
    grads_a(1, 0)
    weight_grads(1, 1)
    grads_a(1, 1)
    d_tokens(1, [xp(2), xp(1)])
    d_cross(2)
    d_cross(1)
    grads_c(0)
    d_tokens(1, [xp(3), x])
    d_cross(3)
    d_cross(0)
    d_merge(2)
    ring_far(*d_ring)
    d_merge(1)
    ring_near(1, *d_ring)
    grads_b(1)
    grads_near(0)
    d_merge(3)
    ring_near(3, *d_ring)
    d_merge(0)
    ring_both(1, d_add, *d_ring)
    ring_both(3, d_add, *d_ring)
    grads_d(0)
    grads_c(1)
    grads_near(1)
    grads_e(0)
    grads_d(1)
    d_inputs()
    grads_e(1)
    w_all = wgt.at[pl.ds(0, 2), pl.ds(0, 4), pl.ds(0, 4), pl.ds(0, 4), pl.ds(0, 240)]
    rows_all = tok.at[pl.ds(0, 4), pl.ds(0, 2), pl.ds(0, 112)]
    sizes = {"w": w_all, "cot": rows_all, "tok": rows_all, "rel": rel.at[zh], "sums": w_all, "dn": rows_all}
    for name, ref in sizes.items():
        net.sent(name, ref, sib)


def write_results(*refs):
    n = len(refs) // 2
    copies = [pltpu.make_async_copy(refs[i], refs[n + i], refs[-1].at[i]) for i in range(n)]
    for copy in copies:
        copy.start()
    for copy in copies:
        copy.wait()


def per_device(inputs, gain, w_query, w_key, w_value, w_out, rel_bias, d_output):
    vmem, anywhere = pl.BlockSpec(memory_space=pltpu.VMEM), pl.BlockSpec(memory_space=pl.ANY)
    grad = jax.ShapeDtypeStruct((256, 256), F32)
    shapes = (jax.ShapeDtypeStruct((128, 2048), BF), grad, grad, grad, grad)
    results = pl.pallas_call(
        kernel,
        out_shape=tuple(pltpu.VMEM(s.shape, s.dtype) for s in shapes),
        in_specs=[anywhere] * 8,
        out_specs=(vmem,) * 5,
        scratch_shapes=[
            pltpu.VMEM((4, 2, 128, 2048), BF),
            pltpu.VMEM((4, 2, 128, 2048), BF),
            pltpu.VMEM((2, 4, 4, 4, 256, 128), BF),
            pltpu.VMEM((2, 8, 128), F32),
            pltpu.VMEM((8, 256, 256), F32),
            pltpu.VMEM((4, 1024, 256), BF),
            pltpu.VMEM((2, 3, 1024, 256), BF),
            pltpu.VMEM((4, 256, 1024), BF),
            pltpu.VMEM((2, 4, 2, 2, 2, 2, 64, 256), BF),
            pltpu.VMEM((2, 4, 2, 2, 4, 64, 256), BF),
            pltpu.VMEM((2, 2, 2, 2, 2, 64, 256), BF),
            pltpu.VMEM((2, 2, 2, 4, 64, 256), BF),
            pltpu.VMEM((2, 2, 2, 2, 2, 2, 64, 256), BF),
            pltpu.VMEM((2, 2, 2, 2, 4, 64, 256), BF),
            pltpu.VMEM((2, 2, 2, 2, 64, 256), BF),
            pltpu.VMEM((2, 2, 2, 2, 2, 64, 256), BF),
            pltpu.VMEM((4, 2, 128, 2048), BF),
            pltpu.VMEM((4, 128, 2048), BF),
            pltpu.VMEM((2, 64, 2048), BF),
            pltpu.VMEM((2, 128, 2048), BF),
            pltpu.VMEM((32, 8, 128), F32),
            pltpu.VMEM((128, 2048), BF),
            pltpu.VMEM((1, 2048), F32),
            pltpu.VMEM((4, 32), F32),
            pltpu.SemaphoreType.DMA((N_SENDS,)),
            pltpu.SemaphoreType.DMA((N_GROUPS,)),
            pltpu.SemaphoreType.DMA((5,)),
        ],
        compiler_params=pltpu.CompilerParams(
            collective_id=0, has_side_effects=True, vmem_limit_bytes=60 * 1024 * 1024
        ),
        name="attention_backward",
    )(inputs, gain.reshape(1, -1), w_query, w_key, w_value, w_out, rel_bias, d_output)
    return pl.pallas_call(
        write_results,
        out_shape=shapes,
        in_specs=[vmem] * 5,
        out_specs=(anywhere,) * 5,
        scratch_shapes=[pltpu.SemaphoreType.DMA((5,))],
        compiler_params=pltpu.CompilerParams(vmem_limit_bytes=8 * 1024 * 1024),
        name="write_results",
    )(*results)


def solution(mesh):
    return jax.shard_map(
        per_device,
        mesh=mesh,
        in_specs=(
            P(("fsdp", "tensor"), None),
            P(),
            P("fsdp", "tensor"),
            P("fsdp", "tensor"),
            P("fsdp", "tensor"),
            P("fsdp", "tensor"),
            P("tensor", None),
            P(("fsdp", "tensor"), None),
        ),
        out_specs=(
            P(("fsdp", "tensor"), None),
            P("fsdp", "tensor"),
            P("fsdp", "tensor"),
            P("fsdp", "tensor"),
            P("fsdp", "tensor"),
        ),
        check_vma=False,
    )
```

```python
import functools

import jax
import jax.numpy as jnp
import numpy as np
from jax import lax
from jax.experimental import pallas as pl
from jax.experimental.pallas import tpu as pltpu
from jax.sharding import PartitionSpec as P

BUCKETS = 32
MAX_DIST = 128
LEN = 256
EPSILON = 1e-06
MESH = pl.DeviceIdType.MESH
BF = jnp.bfloat16
F32 = jnp.float32
OUT, VAL, QRY, KEY = 0, 1, 2, 3


def bucket_steps():
    half_count = BUCKETS // 2
    exact_count = half_count // 2
    distance = np.arange(LEN)
    log_ratio = np.log(np.maximum(distance, 1) / exact_count) / np.log(MAX_DIST / exact_count)
    far = np.minimum(
        exact_count + np.floor(log_ratio * (half_count - exact_count)).astype(np.int64),
        half_count - 1,
    )
    bucket = np.where(distance < exact_count, distance, far)
    return [int(np.argmax(bucket >= k)) for k in range(half_count)]


def dot_nn(a, b):
    return lax.dot_general(a, b, (((1,), (0,)), ((), ())), preferred_element_type=F32)


def dot_nt(a, b):
    return lax.dot_general(a, b, (((1,), (1,)), ((), ())), preferred_element_type=F32)


class Links:
    def __init__(self, send_sem, recv_sem):
        self.send_sem, self.recv_sem = send_sem, recv_sem
        self.groups = {}
        self.sends = {}

    def start(self, group, send, src, dst, peer):
        k = self.groups.setdefault(group, len(self.groups))
        j = self.sends.setdefault(send, len(self.sends))
        pltpu.make_async_remote_copy(
            src_ref=src,
            dst_ref=dst,
            send_sem=self.send_sem.at[j],
            recv_sem=self.recv_sem.at[k],
            device_id=peer,
            device_id_type=MESH,
        ).start()

    def waiter(self, j, k, ref, peer):
        return pltpu.make_async_remote_copy(
            src_ref=ref,
            dst_ref=ref,
            send_sem=self.send_sem.at[j],
            recv_sem=self.recv_sem.at[k],
            device_id=peer,
            device_id_type=MESH,
        )

    def arrived(self, group, ref, peer):
        self.waiter(0, self.groups[group], ref, peer).wait_recv()

    def sent(self, send, ref, peer):
        self.waiter(self.sends[send], 0, ref, peer).wait_send()


N_GROUPS, N_SENDS = 63, 6


def kernel(
    x_in, gain_in, wq_in, wk_in, wv_in, wo_in, rb_in, do_in,
    dx_ref, gq_ref, gk_ref, gv_ref, go_ref,
    tok, cot, wgt, rel, bias, heads, dheads, rows_t,
    part_y, part_z, far_y, far_z, near_y, near_z, far2, near2,
    dn, dn_sib, far_x, near_x, splat, x_ref, gain_ref, rb_ref, send_sem, recv_sem, load_sem,
):
    f, t = lax.axis_index("fsdp"), lax.axis_index("tensor")
    x, zh, c = t // 4, (t // 2) % 2, t % 2
    y, zl = f // 2, f % 2
    z = zh * 2 + zl

    def dev(x, y, z, c):
        return (y * 2 + z % 2, (x * 2 + z // 2) * 2 + c)

    def xp(k):
        return (x + k) % 4

    def yp(k):
        return (y + k) % 4

    def zp(k):
        return (z + k) % 4

    sib = dev(x, y, z, 1 - c)
    to_x = {k: dev(xp(k), y, z, c) for k in (1, 3)}
    to_y = {k: dev(x, yp(k), z, c) for k in (1, 3)}
    to_z = {k: dev(x, y, zp(k), c) for k in (1, 2, 3)}
    peers = [sib] + list(to_x.values()) + list(to_y.values()) + list(to_z.values())
    barrier = pltpu.get_barrier_semaphore()
    for peer in peers:
        pl.semaphore_signal(barrier, inc=1, device_id=peer, device_id_type=MESH)

    loads = [(x_in, x_ref, 0), (gain_in, gain_ref, 1), (rb_in, rb_ref, 2), (do_in, cot.at[x, c], 3)]
    for u in range(2):
        for w, ref in ((OUT, wo_in), (VAL, wv_in), (QRY, wq_in), (KEY, wk_in)):
            loads.append((ref.at[:, pl.ds(u * 128, 128)], wgt.at[u, w, z, y], 4))
    for src, dst, i in loads:
        pltpu.make_async_copy(src, dst, load_sem.at[i]).start()

    def loaded(i, ref):
        pltpu.make_async_copy(ref, ref, load_sem.at[i]).wait()

    net = Links(send_sem, recv_sem)

    def chunk(u, zz, yy, row, n):
        return wgt.at[u, pl.ds(0, 4), zz, yy, pl.ds(row, n)]

    def column(u, zz, row, n):
        return wgt.at[u, pl.ds(0, 4), zz, pl.ds(0, 4), pl.ds(row, n)]

    def line(u, yy, row, n):
        return wgt.at[u, pl.ds(0, 4), pl.ds(0, 4), yy, pl.ds(row, n)]

    def arrived(group, ref):
        net.arrived(group, ref, sib)

    def weights_a(u):
        for part in range(2):
            for k, row in ((1, part * 64), (3, 64 - part * 64)):
                for name, to, at in (("y", to_y, 0), ("z", to_z, 128)):
                    s = chunk(u, z, y, at + row, 64)
                    net.start((name, u) if part else (name, u, k), "w", s, s, to[k])

    def weights_b(u):
        for k, row in ((1, 0), (3, 64)):
            s = chunk(u, z, yp(4 - k), row, 64)
            arrived(("y", u, k), s)
            net.start(("y", u), "w", s, s, to_y[k])
            s = chunk(u, zp(4 - k), y, 128 + row, 64)
            arrived(("z", u, k), s)
            net.start(("z", u), "w", s, s, to_z[k])

    def weights_c(u):
        arrived(("y", u), column(u, z, 0, 64))
        for part in range(2):
            for k, row in ((1, part * 64), (3, 64 - part * 64)):
                s = column(u, z, row, 64)
                net.start(("all", u) if part else ("z2", u, k), "w", s, s, to_z[k])
        arrived(("z", u), line(u, y, 128, 64))
        for part in range(2):
            for k, row in ((1, part * 64), (3, 64 - part * 64)):
                s = line(u, y, 128 + row, 64)
                net.start(("all", u) if part else ("y2", u, k), "w", s, s, to_y[k])

    def weights_d(u):
        for k, row in ((1, 0), (3, 64)):
            s = column(u, zp(4 - k), row, 64)
            arrived(("z2", u, k), s)
            net.start(("all", u), "w", s, s, to_z[k])
            s = line(u, yp(4 - k), 128 + row, 64)
            arrived(("y2", u, k), s)
            net.start(("all", u), "w", s, s, to_y[k])

    def weights_here(u):
        arrived(("all", u), wgt.at[u, pl.ds(0, 4), pl.ds(0, 4), pl.ds(0, 4), pl.ds(0, 128)])

    def tokens_a(name, buf):
        for k in (1, 3):
            net.start((name, k), name, buf.at[x, c], buf.at[x, c], to_x[k])
        net.start("own", name, buf.at[x, c], buf.at[x, c], sib)

    def tokens_b(name, buf):
        for k, row in ((1, 0), (3, 64)):
            arrived((name, k), buf.at[xp(4 - k), c])
            s = buf.at[xp(4 - k), c, pl.ds(row, 64)]
            net.start((name, "far"), name, s, s, to_x[k])
            s = buf.at[xp(4 - k), c]
            net.start("near", name, s, s, sib)

    def tokens_c(name, buf):
        s = buf.at[xp(2), c]
        arrived((name, "far"), s)
        net.start("far", name, s, s, sib)

    def norm_rows(k):
        rows = x_ref[pl.ds(pl.multiple_of(k * 16, 16), 16), :].astype(F32)
        inv = lax.rsqrt(jnp.mean(rows * rows, axis=-1, keepdims=True) + EPSILON)
        return rows * inv, inv

    def normalize():
        @pl.loop(0, 8)
        def _(k):
            unit, _ = norm_rows(k)
            tok[x, c, pl.ds(pl.multiple_of(k * 16, 16), 16), :] = (unit * gain_ref[...]).astype(BF)

    def spread_bias():
        arrived("rel", rel.at[zh])
        steps = bucket_steps()
        table = jnp.concatenate([rel[0, 0:4, :], rel[1, 0:4, :]], axis=0)
        for k in range(BUCKETS):
            splat[k] = jnp.broadcast_to(table[:, k : k + 1], (8, 128))

        @pl.loop(0, LEN // 8)
        def _(k):
            i = lax.broadcasted_iota(jnp.int32, (8, LEN), 0) + k * 8
            r = lax.broadcasted_iota(jnp.int32, (8, LEN), 1) - i

            def row(b, h):
                return jnp.broadcast_to(splat[b, h : h + 1, 0:1], (8, LEN))

            values = [row(0, h) for h in range(8)]
            for b in range(1, BUCKETS // 2):
                for chosen, at in ((r <= -steps[b], b), (r >= steps[b], BUCKETS // 2 + b)):
                    for h in range(8):
                        values[h] = jnp.where(chosen, row(at, h), values[h])
            for h in range(8):
                bias[h, pl.ds(pl.multiple_of(k * 8, 8), 8), :] = values[h]

    lane = lax.broadcasted_iota(jnp.int32, (1, 128), 1)
    mask = [(lane < 64).astype(F32).astype(BF), (lane >= 64).astype(F32).astype(BF)]
    row_at = lax.broadcasted_iota(jnp.int32, (128, 1), 0)
    mask_t = [(row_at < 64).astype(F32).astype(BF), (row_at >= 64).astype(F32).astype(BF)]

    def passages(u, places):
        n = len(places)

        def by_chunk(buf):
            whole = jnp.concatenate([buf[p].reshape(256, 2048) for p in places], axis=0)
            order = [yy * 2 + zz for zz in range(2) for yy in range(4)]
            return jnp.concatenate([whole[:, i * 256 : i * 256 + 256] for i in order], axis=1)

        for w in range(4):
            left = by_chunk(cot if w == OUT else tok)
            right = jnp.concatenate([wgt[u, w, g * 2 : g * 2 + 2].reshape(2048, 128) for g in range(2)], axis=1)
            heads[w, 0 : n * 256] = dot_nn(left, right).astype(BF)
        for i, p in enumerate(places):
            attention(u, i, pl.ds(pl.multiple_of(p * 256, 256), 256))

    def attention(u, i, rows):
        parts = [
            tuple(heads[w, i * 256 : i * 256 + 256, g * 128 : g * 128 + 128] for w in range(4)) for g in range(2)
        ]
        scores = [
            [dot_nt(q2 * mask[h], k2) + bias[g * 4 + u * 2 + h] for h in range(2)]
            for g, (_, _, q2, k2) in enumerate(parts)
        ]
        d_prob = [[dot_nt(dc2 * mask[h], v2) for h in range(2)] for dc2, v2, _, _ in parts]
        probs_b, d_score = [[], []], [[], []]
        for g in range(2):
            for h in range(2):
                e = jnp.exp(scores[g][h] - jnp.max(scores[g][h], axis=-1, keepdims=True))
                probs = e * (1.0 / jnp.sum(e, axis=-1, keepdims=True))
                row_dot = jnp.sum(probs * d_prob[g][h], axis=-1, keepdims=True)
                probs_b[g].append(probs.astype(BF))
                d_score[g].append((probs * (d_prob[g][h] - row_dot)).astype(BF))
        for g, (dc2, v2, q2, k2) in enumerate(parts):
            ctx = dot_nn(
                jnp.concatenate(probs_b[g], axis=1),
                jnp.concatenate([v2 * mask[0], v2 * mask[1]], axis=0),
            ).astype(BF)
            dq = dot_nn(
                jnp.concatenate(d_score[g], axis=1),
                jnp.concatenate([k2 * mask[0], k2 * mask[1]], axis=0),
            ).astype(BF)
            dc_t, q_t = dc2.T, q2.T
            dv_t = dot_nn(
                jnp.concatenate([dc_t * mask_t[0], dc_t * mask_t[1]], axis=1),
                jnp.concatenate(probs_b[g], axis=0),
            ).astype(BF)
            dk_t = dot_nn(
                jnp.concatenate([q_t * mask_t[0], q_t * mask_t[1]], axis=1),
                jnp.concatenate(d_score[g], axis=0),
            ).astype(BF)
            at, lanes = pl.ds(g * 128, 128), pl.ds(g * 128, 128)
            rows_t[u, OUT, at, rows] = ctx.T
            rows_t[u, VAL, at, rows] = dv_t
            rows_t[u, QRY, at, rows] = dq.T
            rows_t[u, KEY, at, rows] = dk_t
            dheads[u, VAL - 1, rows, lanes] = dv_t.T
            dheads[u, QRY - 1, rows, lanes] = dq
            dheads[u, KEY - 1, rows, lanes] = dk_t.T

    def weight_grads(u, k):
        cols = pl.ds(pl.multiple_of(yp(k) * 512, 512), 512)
        for w, buf in ((OUT, cot), (VAL, tok)):
            res = dot_nn(rows_t[u, w], buf[:, :, :, cols].reshape(1024, 512)).astype(BF)
            for g in range(2):
                for h in range(2):
                    at = g * 128 + h * 64
                    for fz in range(2):
                        part_y[u, yp(k), h, w, g, fz] = res[at : at + 64, fz * 256 : fz * 256 + 256]
        rows = pl.ds(pl.multiple_of(zp(k) // 2 * 128, 128), 128)
        left = jnp.concatenate([rows_t[u, w, rows] for w in (QRY, KEY)], axis=0)
        starts = [pl.multiple_of((fy * 2 + zp(k) % 2) * 256, 256) for fy in range(4)]
        right = jnp.concatenate([tok[:, :, :, pl.ds(at, 256)].reshape(1024, 256) for at in starts], axis=1)
        res = dot_nn(left, right).astype(BF)
        for w in range(2):
            for h in range(2):
                at = w * 128 + h * 64
                for fy in range(4):
                    part_z[u, zp(k), h, w, fy] = res[at : at + 64, fy * 256 : fy * 256 + 256]

    def ring_far(key, block, far, near, to, send):
        net.start((key, 1), send, block(2, 0), far(0), to[1])
        net.start((key, 3), send, block(2, 1), far(1), to[3])

    def ring_near(k, key, block, far, near, to, send):
        half, side = (1, 0) if k == 1 else (0, 1)
        net.start(key, send, block(k, half), near(side, half), to[k])

    def ring_both(k, add, key, block, far, near, to, send):
        half, side = (0, 0) if k == 1 else (1, 1)
        arrived((key, k), far(side))
        add(block(k, half), far(side))
        net.start(key, send, block(k, half), near(side, half), to[k])

    def add_into(dst, src):
        dst[...] = (dst[...].astype(F32) + src[...].astype(F32)).astype(BF)

    def add_pair(dst, src):
        for w in range(2):
            add_into(dst.at[w], src.at[w])

    def first(u, pair):
        if pair == 0:
            return (
                ("s1", u, pair),
                lambda k, h: part_y.at[u, yp(k), h],
                lambda s: far_y.at[u, s],
                lambda s, h: near_y.at[u, s, h],
                to_y,
                "sums",
            )
        return (
            ("s1", u, pair),
            lambda k, h: part_z.at[u, zp(k), h],
            lambda s: far_z.at[u, s],
            lambda s, h: near_z.at[u, s, h],
            to_z,
            "sums",
        )

    def second(u, pair):
        def block(k, h):
            if pair == 0:
                return part_y.at[u, y, h, pl.ds(0, 2), zp(k) // 2, zp(k) % 2]
            return part_z.at[u, z, h, pl.ds(0, 2), yp(k)]

        return (
            ("s2", u, pair),
            block,
            lambda s: far2.at[u, pair, s],
            lambda s, h: near2.at[u, pair, s, h],
            to_z if pair == 0 else to_y,
            "sums",
        )

    def grads_far(u):
        for pair in range(2):
            ring_far(*first(u, pair))

    def grads_next(u, k):
        for pair in range(2):
            ring_near(k, *first(u, pair))

    def grads_b(u):
        for k in (1, 3):
            for pair in range(2):
                ring_both(k, add_pair, *first(u, pair))

    def grads_c(u):
        for pair in range(2):
            own, near = (part_y.at[u, y], near_y.at[u]) if pair == 0 else (part_z.at[u, z], near_z.at[u])
            arrived(("s1", u, pair), near)
            for h in range(2):
                for w in range(2):
                    total = own[h, w].astype(F32) + near[0, h, w].astype(F32) + near[1, h, w].astype(F32)
                    own[h, w] = total.astype(BF)
            ring_far(*second(u, pair))

    def grads_near(u):
        for pair in range(2):
            for k in (1, 3):
                ring_near(k, *second(u, pair))

    def grads_d(u):
        for k in (1, 3):
            for pair in range(2):
                ring_both(k, add_into, *second(u, pair))

    def grads_e(u):
        for pair, outs in ((0, (go_ref, gv_ref)), (1, (gq_ref, gk_ref))):
            near = near2.at[u, pair]
            arrived(("s2", u, pair), near)
            for w in range(2):
                for h in range(2):
                    own = part_y[u, y, h, w, zh, zl] if pair == 0 else part_z[u, z, h, w, y]
                    total = own.astype(F32) + near[0, h, w].astype(F32) + near[1, h, w].astype(F32)
                    outs[w][:, u * 128 + h * 64 : u * 128 + h * 64 + 64] = total.T

    def d_tokens(u, places):
        pieces = [(w, g) for w in range(3) for g in range(2)]
        left = jnp.concatenate(
            [
                jnp.concatenate([dheads[u, w, pl.ds(pl.multiple_of(p * 256, 256), 256), :] for w in range(3)], axis=1)
                for p in places
            ],
            axis=0,
        )
        for f in range(8):
            cols = pl.ds(f * 256, 256)
            right = jnp.concatenate([wgt[u, w + 1, g * 2 + f % 2, f // 2] for w, g in pieces], axis=1)
            total = dot_nt(left, right)
            for i, p in enumerate(places):
                block = total[i * 256 : i * 256 + 256].reshape(2, 128, 256)
                if u:
                    block = block + dn[p, :, :, cols].astype(F32)
                dn[p, :, :, cols] = block.astype(BF)

    def d_cross(k):
        net.start(("cross", k), "dn", dn.at[xp(k), 1 - c], dn_sib.at[xp(k)], sib)

    def add_rows(dst, src, n):
        @pl.loop(0, n // 16)
        def _(m):
            rows = pl.ds(pl.multiple_of(m * 16, 16), 16)
            dst[rows, :] = (dst[rows, :].astype(F32) + src[rows, :].astype(F32)).astype(BF)

    def d_merge(k):
        arrived(("cross", k), dn_sib.at[xp(k)])
        add_rows(dn.at[xp(k), c], dn_sib.at[xp(k)], 128)

    d_ring = (
        "dx",
        lambda k, h: dn.at[xp(k), c, pl.ds(h * 64, 64)],
        lambda s: far_x.at[s],
        lambda s, h: near_x.at[s, pl.ds(h * 64, 64)],
        to_x,
        "dn",
    )

    def d_inputs():
        arrived("dx", near_x)

        @pl.loop(0, 8)
        def _(m):
            rows = pl.ds(pl.multiple_of(m * 16, 16), 16)
            unit, inv = norm_rows(m)
            d_normed = dn[x, c, rows, :].astype(F32) + near_x[0, rows, :].astype(F32) + near_x[1, rows, :].astype(F32)
            d_unit = d_normed * gain_ref[...]
            branch = inv * (d_unit - unit * jnp.mean(d_unit * unit, axis=-1, keepdims=True))
            dx_ref[rows, :] = (cot[x, c, rows, :].astype(F32) + branch).astype(BF)

    def d_add(dst, src):
        add_rows(dst, src, 64)

    loaded(2, rb_ref)
    rel[zh] = jnp.zeros((8, 128), F32)
    rel[zh, 0:4, 0:32] = rb_ref[...]
    loaded(0, x_ref)
    loaded(1, gain_ref)
    normalize()
    loaded(3, cot.at[x, c])
    loaded(4, wgt.at[pl.ds(0, 2), pl.ds(0, 4), z, y])
    pl.semaphore_wait(barrier, len(peers))
    weights_a(0)
    tokens_a("cot", cot)
    tokens_a("tok", tok)
    net.start("rel", "rel", rel.at[zh], rel.at[zh], to_z[2])
    weights_b(0)
    weights_a(1)
    weights_c(0)
    weights_b(1)
    spread_bias()
    weights_d(0)
    tokens_b("cot", cot)
    weights_c(1)
    tokens_b("tok", tok)
    weights_here(0)
    arrived("own", tok.at[pl.ds(0, 2), 0])
    passages(0, [x])
    arrived("near", tok.at[pl.ds(0, 4), 0])
    tokens_c("cot", cot)
    passages(0, [xp(1)])
    weights_d(1)
    tokens_c("tok", tok)
    passages(0, [xp(3)])
    arrived("far", tok.at[pl.ds(0, 2), 0])
    passages(0, [xp(2)])
    weight_grads(0, 2)
    grads_far(0)
    for k in (1, 3):
        weight_grads(0, k)
        grads_next(0, k)
    d_tokens(0, [xp(2), xp(1), xp(3)])
    weights_here(1)
    passages(1, [0, 1])
    grads_b(0)
    passages(1, [2, 3])
    weight_grads(1, 2)
    grads_far(1)
    d_tokens(1, [xp(2)])
    d_cross(2)
    for k in (1, 3):
        weight_grads(1, k)
        grads_next(1, k)
    d_merge(2)
    ring_far(*d_ring)
    d_tokens(1, [xp(1), xp(3)])
    d_cross(1)
    d_cross(3)
    weight_grads(0, 0)
    d_merge(1)
    ring_near(1, *d_ring)
    d_merge(3)
    ring_near(3, *d_ring)
    grads_c(0)
    grads_b(1)
    grads_near(0)
    weight_grads(1, 0)
    ring_both(1, d_add, *d_ring)
    ring_both(3, d_add, *d_ring)
    d_tokens(0, [x])
    d_tokens(1, [x])
    d_cross(0)
    grads_d(0)
    d_merge(0)
    grads_c(1)
    grads_near(1)
    grads_e(0)
    grads_d(1)
    d_inputs()
    grads_e(1)
    w_all = wgt.at[pl.ds(0, 2), pl.ds(0, 4), pl.ds(0, 4), pl.ds(0, 4), pl.ds(0, 240)]
    rows_all = tok.at[pl.ds(0, 4), pl.ds(0, 2), pl.ds(0, 112)]
    sizes = {"w": w_all, "cot": rows_all, "tok": rows_all, "rel": rel.at[zh], "sums": w_all, "dn": rows_all}
    for name, ref in sizes.items():
        net.sent(name, ref, sib)


def write_results(*refs):
    n = len(refs) // 2
    copies = [pltpu.make_async_copy(refs[i], refs[n + i], refs[-1].at[i]) for i in range(n)]
    for copy in copies:
        copy.start()
    for copy in copies:
        copy.wait()


def per_device(inputs, gain, w_query, w_key, w_value, w_out, rel_bias, d_output):
    vmem, anywhere = pl.BlockSpec(memory_space=pltpu.VMEM), pl.BlockSpec(memory_space=pl.ANY)
    grad = jax.ShapeDtypeStruct((256, 256), F32)
    shapes = (jax.ShapeDtypeStruct((128, 2048), BF), grad, grad, grad, grad)
    results = pl.pallas_call(
        kernel,
        out_shape=tuple(pltpu.VMEM(s.shape, s.dtype) for s in shapes),
        in_specs=[anywhere] * 8,
        out_specs=(vmem,) * 5,
        scratch_shapes=[
            pltpu.VMEM((4, 2, 128, 2048), BF),
            pltpu.VMEM((4, 2, 128, 2048), BF),
            pltpu.VMEM((2, 4, 4, 4, 256, 128), BF),
            pltpu.VMEM((2, 8, 128), F32),
            pltpu.VMEM((8, 256, 256), F32),
            pltpu.VMEM((4, 1024, 256), BF),
            pltpu.VMEM((2, 3, 1024, 256), BF),
            pltpu.VMEM((2, 4, 256, 1024), BF),
            pltpu.VMEM((2, 4, 2, 2, 2, 2, 64, 256), BF),
            pltpu.VMEM((2, 4, 2, 2, 4, 64, 256), BF),
            pltpu.VMEM((2, 2, 2, 2, 2, 64, 256), BF),
            pltpu.VMEM((2, 2, 2, 4, 64, 256), BF),
            pltpu.VMEM((2, 2, 2, 2, 2, 2, 64, 256), BF),
            pltpu.VMEM((2, 2, 2, 2, 4, 64, 256), BF),
            pltpu.VMEM((2, 2, 2, 2, 64, 256), BF),
            pltpu.VMEM((2, 2, 2, 2, 2, 64, 256), BF),
            pltpu.VMEM((4, 2, 128, 2048), BF),
            pltpu.VMEM((4, 128, 2048), BF),
            pltpu.VMEM((2, 64, 2048), BF),
            pltpu.VMEM((2, 128, 2048), BF),
            pltpu.VMEM((32, 8, 128), F32),
            pltpu.VMEM((128, 2048), BF),
            pltpu.VMEM((1, 2048), F32),
            pltpu.VMEM((4, 32), F32),
            pltpu.SemaphoreType.DMA((N_SENDS,)),
            pltpu.SemaphoreType.DMA((N_GROUPS,)),
            pltpu.SemaphoreType.DMA((5,)),
        ],
        compiler_params=pltpu.CompilerParams(
            collective_id=0, has_side_effects=True, vmem_limit_bytes=60 * 1024 * 1024
        ),
        name="attention_backward",
    )(inputs, gain.reshape(1, -1), w_query, w_key, w_value, w_out, rel_bias, d_output)
    return pl.pallas_call(
        write_results,
        out_shape=shapes,
        in_specs=[vmem] * 5,
        out_specs=(anywhere,) * 5,
        scratch_shapes=[pltpu.SemaphoreType.DMA((5,))],
        compiler_params=pltpu.CompilerParams(vmem_limit_bytes=8 * 1024 * 1024),
        name="write_results",
    )(*results)


def solution(mesh):
    return jax.shard_map(
        per_device,
        mesh=mesh,
        in_specs=(
            P(("fsdp", "tensor"), None),
            P(),
            P("fsdp", "tensor"),
            P("fsdp", "tensor"),
            P("fsdp", "tensor"),
            P("fsdp", "tensor"),
            P("tensor", None),
            P(("fsdp", "tensor"), None),
        ),
        out_specs=(
            P(("fsdp", "tensor"), None),
            P("fsdp", "tensor"),
            P("fsdp", "tensor"),
            P("fsdp", "tensor"),
            P("fsdp", "tensor"),
        ),
        check_vma=False,
    )
```

```python
import functools

import jax
import jax.numpy as jnp
import numpy as np
from jax import lax
from jax.experimental import pallas as pl
from jax.experimental.pallas import tpu as pltpu
from jax.sharding import PartitionSpec as P

BUCKETS = 32
MAX_DIST = 128
LEN = 256
EPSILON = 1e-06
MESH = pl.DeviceIdType.MESH
BF = jnp.bfloat16
F32 = jnp.float32
OUT, VAL, QRY, KEY = 0, 1, 2, 3


def bucket_steps():
    half_count = BUCKETS // 2
    exact_count = half_count // 2
    distance = np.arange(LEN)
    log_ratio = np.log(np.maximum(distance, 1) / exact_count) / np.log(MAX_DIST / exact_count)
    far = np.minimum(
        exact_count + np.floor(log_ratio * (half_count - exact_count)).astype(np.int64),
        half_count - 1,
    )
    bucket = np.where(distance < exact_count, distance, far)
    return [int(np.argmax(bucket >= k)) for k in range(half_count)]


def dot_nn(a, b):
    return lax.dot_general(a, b, (((1,), (0,)), ((), ())), preferred_element_type=F32)


def dot_nt(a, b):
    return lax.dot_general(a, b, (((1,), (1,)), ((), ())), preferred_element_type=F32)


class Links:
    def __init__(self, send_sem, recv_sem):
        self.send_sem, self.recv_sem = send_sem, recv_sem
        self.groups = {}
        self.sends = {}

    def start(self, group, send, src, dst, peer):
        k = self.groups.setdefault(group, len(self.groups))
        j = self.sends.setdefault(send, len(self.sends))
        pltpu.make_async_remote_copy(
            src_ref=src,
            dst_ref=dst,
            send_sem=self.send_sem.at[j],
            recv_sem=self.recv_sem.at[k],
            device_id=peer,
            device_id_type=MESH,
        ).start()

    def waiter(self, j, k, ref, peer):
        return pltpu.make_async_remote_copy(
            src_ref=ref,
            dst_ref=ref,
            send_sem=self.send_sem.at[j],
            recv_sem=self.recv_sem.at[k],
            device_id=peer,
            device_id_type=MESH,
        )

    def arrived(self, group, ref, peer):
        self.waiter(0, self.groups[group], ref, peer).wait_recv()

    def sent(self, send, ref, peer):
        self.waiter(self.sends[send], 0, ref, peer).wait_send()


N_GROUPS, N_SENDS = 75, 6


def kernel(
    x_in, gain_in, wq_in, wk_in, wv_in, wo_in, rb_in, do_in,
    dx_ref, gq_ref, gk_ref, gv_ref, go_ref,
    tok, cot, wgt, rel, bias, heads, dheads, rows_t,
    part_y, part_z, far_y, far_z, near_y, near_z, far2, near2,
    dn, dn_sib, far_x, near_x, splat, x_ref, gain_ref, rb_ref, send_sem, recv_sem, load_sem,
):
    f, t = lax.axis_index("fsdp"), lax.axis_index("tensor")
    x, zh, c = t // 4, (t // 2) % 2, t % 2
    y, zl = f // 2, f % 2
    z = zh * 2 + zl

    def dev(x, y, z, c):
        return (y * 2 + z % 2, (x * 2 + z // 2) * 2 + c)

    def xp(k):
        return (x + k) % 4

    def yp(k):
        return (y + k) % 4

    def zp(k):
        return (z + k) % 4

    sib = dev(x, y, z, 1 - c)
    to_x = {k: dev(xp(k), y, z, c) for k in (1, 3)}
    to_y = {k: dev(x, yp(k), z, c) for k in (1, 3)}
    to_z = {k: dev(x, y, zp(k), c) for k in (1, 2, 3)}
    peers = [sib] + list(to_x.values()) + list(to_y.values()) + list(to_z.values())
    barrier = pltpu.get_barrier_semaphore()
    for peer in peers:
        pl.semaphore_signal(barrier, inc=1, device_id=peer, device_id_type=MESH)

    loads = [(x_in, x_ref, 0), (gain_in, gain_ref, 1), (rb_in, rb_ref, 2), (do_in, cot.at[x, c], 3)]
    for u in range(2):
        for w, ref in ((OUT, wo_in), (VAL, wv_in), (QRY, wq_in), (KEY, wk_in)):
            loads.append((ref.at[:, pl.ds(u * 128, 128)], wgt.at[u, w, z, y], 4))
    for src, dst, i in loads:
        pltpu.make_async_copy(src, dst, load_sem.at[i]).start()

    def loaded(i, ref):
        pltpu.make_async_copy(ref, ref, load_sem.at[i]).wait()

    net = Links(send_sem, recv_sem)

    def chunk(u, zz, yy, row, n):
        return wgt.at[u, pl.ds(0, 4), zz, yy, pl.ds(row, n)]

    def column(u, zz, row, n):
        return wgt.at[u, pl.ds(0, 4), zz, pl.ds(0, 4), pl.ds(row, n)]

    def line(u, yy, row, n):
        return wgt.at[u, pl.ds(0, 4), pl.ds(0, 4), yy, pl.ds(row, n)]

    def arrived(group, ref):
        net.arrived(group, ref, sib)

    def weights_a(u):
        for part in range(2):
            for k, row in ((1, part * 64), (3, 64 - part * 64)):
                for name, to, at in (("y", to_y, 0), ("z", to_z, 128)):
                    s = chunk(u, z, y, at + row, 64)
                    net.start((name, u) if part else (name, u, k), "w", s, s, to[k])

    def weights_b(u):
        for k, row in ((1, 0), (3, 64)):
            s = chunk(u, z, yp(4 - k), row, 64)
            arrived(("y", u, k), s)
            net.start(("y", u), "w", s, s, to_y[k])
            s = chunk(u, zp(4 - k), y, 128 + row, 64)
            arrived(("z", u, k), s)
            net.start(("z", u), "w", s, s, to_z[k])

    def weights_c(u):
        arrived(("y", u), column(u, z, 0, 64))
        for part in range(2):
            for k, row in ((1, part * 64), (3, 64 - part * 64)):
                s = column(u, z, row, 64)
                net.start(("all", u) if part else ("z2", u, k), "w", s, s, to_z[k])
        arrived(("z", u), line(u, y, 128, 64))
        for part in range(2):
            for k, row in ((1, part * 64), (3, 64 - part * 64)):
                s = line(u, y, 128 + row, 64)
                net.start(("all", u) if part else ("y2", u, k), "w", s, s, to_y[k])

    def weights_d(u):
        for k, row in ((1, 0), (3, 64)):
            s = column(u, zp(4 - k), row, 64)
            arrived(("z2", u, k), s)
            net.start(("all", u), "w", s, s, to_z[k])
            s = line(u, yp(4 - k), 128 + row, 64)
            arrived(("y2", u, k), s)
            net.start(("all", u), "w", s, s, to_y[k])

    def weights_here(u):
        arrived(("all", u), wgt.at[u, pl.ds(0, 4), pl.ds(0, 4), pl.ds(0, 4), pl.ds(0, 128)])

    def tokens_a(name, buf):
        for k in (1, 3):
            net.start((name, k), name, buf.at[x, c], buf.at[x, c], to_x[k])
        net.start("own", name, buf.at[x, c], buf.at[x, c], sib)

    def tokens_b(name, buf):
        for k, row in ((1, 0), (3, 64)):
            arrived((name, k), buf.at[xp(4 - k), c])
            s = buf.at[xp(4 - k), c, pl.ds(row, 64)]
            net.start((name, "far"), name, s, s, to_x[k])
            s = buf.at[xp(4 - k), c]
            net.start("near", name, s, s, sib)

    def tokens_c(name, buf):
        s = buf.at[xp(2), c]
        arrived((name, "far"), s)
        net.start("far", name, s, s, sib)

    def norm_rows(k):
        rows = x_ref[pl.ds(pl.multiple_of(k * 16, 16), 16), :].astype(F32)
        inv = lax.rsqrt(jnp.mean(rows * rows, axis=-1, keepdims=True) + EPSILON)
        return rows * inv, inv

    def normalize():
        @pl.loop(0, 8)
        def _(k):
            unit, _ = norm_rows(k)
            tok[x, c, pl.ds(pl.multiple_of(k * 16, 16), 16), :] = (unit * gain_ref[...]).astype(BF)

    def spread_bias():
        arrived("rel", rel.at[zh])
        steps = bucket_steps()
        table = jnp.concatenate([rel[0, 0:4, :], rel[1, 0:4, :]], axis=0)
        for k in range(BUCKETS):
            splat[k] = jnp.broadcast_to(table[:, k : k + 1], (8, 128))

        @pl.loop(0, LEN // 8)
        def _(k):
            i = lax.broadcasted_iota(jnp.int32, (8, LEN), 0) + k * 8
            r = lax.broadcasted_iota(jnp.int32, (8, LEN), 1) - i

            def row(b, h):
                return jnp.broadcast_to(splat[b, h : h + 1, 0:1], (8, LEN))

            values = [row(0, h) for h in range(8)]
            for b in range(1, BUCKETS // 2):
                for chosen, at in ((r <= -steps[b], b), (r >= steps[b], BUCKETS // 2 + b)):
                    for h in range(8):
                        values[h] = jnp.where(chosen, row(at, h), values[h])
            for h in range(8):
                bias[h, pl.ds(pl.multiple_of(k * 8, 8), 8), :] = values[h]

    lane = lax.broadcasted_iota(jnp.int32, (1, 128), 1)
    mask = [(lane < 64).astype(F32).astype(BF), (lane >= 64).astype(F32).astype(BF)]
    row_at = lax.broadcasted_iota(jnp.int32, (128, 1), 0)
    mask_t = [(row_at < 64).astype(F32).astype(BF), (row_at >= 64).astype(F32).astype(BF)]

    def passages(u, places):
        n = len(places)

        def by_chunk(buf):
            whole = jnp.concatenate([buf[p].reshape(256, 2048) for p in places], axis=0)
            order = [yy * 2 + zz for zz in range(2) for yy in range(4)]
            return jnp.concatenate([whole[:, i * 256 : i * 256 + 256] for i in order], axis=1)

        for w in range(4):
            left = by_chunk(cot if w == OUT else tok)
            right = jnp.concatenate([wgt[u, w, g * 2 : g * 2 + 2].reshape(2048, 128) for g in range(2)], axis=1)
            heads[w, 0 : n * 256] = dot_nn(left, right).astype(BF)
        for i, p in enumerate(places):
            attention(u, i, pl.ds(pl.multiple_of(p * 256, 256), 256))

    def attention(u, i, rows):
        parts = [
            tuple(heads[w, i * 256 : i * 256 + 256, g * 128 : g * 128 + 128] for w in range(4)) for g in range(2)
        ]
        scores = [
            [dot_nt(q2 * mask[h], k2) + bias[g * 4 + u * 2 + h] for h in range(2)]
            for g, (_, _, q2, k2) in enumerate(parts)
        ]
        d_prob = [[dot_nt(dc2 * mask[h], v2) for h in range(2)] for dc2, v2, _, _ in parts]
        probs_b, d_score = [[], []], [[], []]
        for g in range(2):
            for h in range(2):
                e = jnp.exp(scores[g][h] - jnp.max(scores[g][h], axis=-1, keepdims=True))
                probs = e * (1.0 / jnp.sum(e, axis=-1, keepdims=True))
                row_dot = jnp.sum(probs * d_prob[g][h], axis=-1, keepdims=True)
                probs_b[g].append(probs.astype(BF))
                d_score[g].append((probs * (d_prob[g][h] - row_dot)).astype(BF))
        for g, (dc2, v2, q2, k2) in enumerate(parts):
            ctx = dot_nn(
                jnp.concatenate(probs_b[g], axis=1),
                jnp.concatenate([v2 * mask[0], v2 * mask[1]], axis=0),
            ).astype(BF)
            dq = dot_nn(
                jnp.concatenate(d_score[g], axis=1),
                jnp.concatenate([k2 * mask[0], k2 * mask[1]], axis=0),
            ).astype(BF)
            dc_t, q_t = dc2.T, q2.T
            dv_t = dot_nn(
                jnp.concatenate([dc_t * mask_t[0], dc_t * mask_t[1]], axis=1),
                jnp.concatenate(probs_b[g], axis=0),
            ).astype(BF)
            dk_t = dot_nn(
                jnp.concatenate([q_t * mask_t[0], q_t * mask_t[1]], axis=1),
                jnp.concatenate(d_score[g], axis=0),
            ).astype(BF)
            at, lanes = pl.ds(g * 128, 128), pl.ds(g * 128, 128)
            rows_t[u, OUT, at, rows] = ctx.T
            rows_t[u, VAL, at, rows] = dv_t
            rows_t[u, QRY, at, rows] = dq.T
            rows_t[u, KEY, at, rows] = dk_t
            dheads[u, VAL - 1, rows, lanes] = dv_t.T
            dheads[u, QRY - 1, rows, lanes] = dq
            dheads[u, KEY - 1, rows, lanes] = dk_t.T

    def weight_grads(u, k):
        cols = pl.ds(pl.multiple_of(yp(k) * 512, 512), 512)
        for w, buf in ((OUT, cot), (VAL, tok)):
            res = dot_nn(rows_t[u, w], buf[:, :, :, cols].reshape(1024, 512)).astype(BF)
            for g in range(2):
                for h in range(2):
                    at = g * 128 + h * 64
                    for fz in range(2):
                        part_y[u, yp(k), h, w, g, fz] = res[at : at + 64, fz * 256 : fz * 256 + 256]
        rows = pl.ds(pl.multiple_of(zp(k) // 2 * 128, 128), 128)
        left = jnp.concatenate([rows_t[u, w, rows] for w in (QRY, KEY)], axis=0)
        starts = [pl.multiple_of((fy * 2 + zp(k) % 2) * 256, 256) for fy in range(4)]
        right = jnp.concatenate([tok[:, :, :, pl.ds(at, 256)].reshape(1024, 256) for at in starts], axis=1)
        res = dot_nn(left, right).astype(BF)
        for w in range(2):
            for h in range(2):
                at = w * 128 + h * 64
                for fy in range(4):
                    part_z[u, zp(k), h, w, fy] = res[at : at + 64, fy * 256 : fy * 256 + 256]

    def ring_far(key, block, far, near, to, send):
        net.start((key, "far", 1), send, block(2, 0), far(0), to[1])
        net.start((key, "far", 3), send, block(2, 1), far(1), to[3])

    def ring_near(k, group, key, block, far, near, to, send):
        half, side = (1, 0) if k == 1 else (0, 1)
        net.start(group, send, block(k, half), near(side, half), to[k])

    def ring_both(k, group, key, block, far, near, to, send):
        half, side = (0, 0) if k == 1 else (1, 1)
        net.start(group, send, block(k, half), near(side, half), to[k])

    def ring_add(k, add, key, block, far, near, to, send):
        half, side = (0, 0) if k == 1 else (1, 1)
        arrived((key, "far", k), far(side))
        add(block(k, half), far(side))

    def add_into(dst, src):
        dst[...] = (dst[...].astype(F32) + src[...].astype(F32)).astype(BF)

    def add_each(dst, src):
        for w in range(dst.shape[0]):
            add_into(dst.at[w], src.at[w])

    splits = {0: [(0, 2)], 1: [(0, 1), (1, 1)]}

    def first(u, pair, start=0, n=2):
        ws = pl.ds(start, n)
        if pair == 0:
            return (
                ("s1", u, pair),
                lambda k, h: part_y.at[u, yp(k), h, ws],
                lambda s: far_y.at[u, s, ws],
                lambda s, h: near_y.at[u, s, h, ws],
                to_y,
                "sums",
            )
        return (
            ("s1", u, pair),
            lambda k, h: part_z.at[u, zp(k), h, ws],
            lambda s: far_z.at[u, s, ws],
            lambda s, h: near_z.at[u, s, h, ws],
            to_z,
            "sums",
        )

    def second(u, pair, start, n):
        ws = pl.ds(start, n)

        def block(k, h):
            if pair == 0:
                return part_y.at[u, y, h, ws, zp(k) // 2, zp(k) % 2]
            return part_z.at[u, z, h, ws, yp(k)]

        return (
            ("s2", u, pair, start),
            block,
            lambda s: far2.at[u, pair, s, ws],
            lambda s, h: near2.at[u, pair, s, h, ws],
            to_z if pair == 0 else to_y,
            "sums",
        )

    def grads_far(u):
        for pair in range(2):
            ring_far(*first(u, pair))

    def grads_next(u, k):
        for pair in range(2):
            ring_near(k, ("s1n", u, pair), *first(u, pair))

    def grads_b(u):
        for k in (1, 3):
            for pair in range(2):
                ring_add(k, add_each, *first(u, pair))
                start, n = splits[u][0]
                ring_both(k, ("s1b", u, pair, start), *first(u, pair, start, n))
        for start, n in splits[u][1:]:
            for k in (1, 3):
                for pair in range(2):
                    ring_both(k, ("s1b", u, pair, start), *first(u, pair, start, n))

    def grads_c(u, part):
        start, n = splits[u][part]
        for pair in range(2):
            own, near = (part_y.at[u, y], near_y.at[u]) if pair == 0 else (part_z.at[u, z], near_z.at[u])
            if part == 0:
                arrived(("s1n", u, pair), near.at[0])
            arrived(("s1b", u, pair, start), near.at[0] if n == 2 else near.at[0, 0])
            for h in range(2):
                for w in range(start, start + n):
                    total = own[h, w].astype(F32) + near[0, h, w].astype(F32) + near[1, h, w].astype(F32)
                    own[h, w] = total.astype(BF)
            ring_far(*second(u, pair, start, n))

    def grads_near(u, part):
        for pair in range(2):
            for k in (1, 3):
                args = second(u, pair, *splits[u][part])
                ring_near(k, args[0], *args)

    def grads_d(u, part):
        for k in (1, 3):
            for pair in range(2):
                args = second(u, pair, *splits[u][part])
                ring_add(k, add_into, *args)
                ring_both(k, args[0], *args)

    def grads_e(u):
        for pair, outs in ((0, (go_ref, gv_ref)), (1, (gq_ref, gk_ref))):
            near = near2.at[u, pair]
            for start, n in splits[u]:
                arrived(("s2", u, pair, start), near if n == 2 else near.at[0])
            for w in range(2):
                for h in range(2):
                    own = part_y[u, y, h, w, zh, zl] if pair == 0 else part_z[u, z, h, w, y]
                    total = own.astype(F32) + near[0, h, w].astype(F32) + near[1, h, w].astype(F32)
                    outs[w][:, u * 128 + h * 64 : u * 128 + h * 64 + 64] = total.T

    def d_tokens(u, places):
        pieces = [(w, g) for w in range(3) for g in range(2)]
        left = jnp.concatenate(
            [
                jnp.concatenate([dheads[u, w, pl.ds(pl.multiple_of(p * 256, 256), 256), :] for w in range(3)], axis=1)
                for p in places
            ],
            axis=0,
        )
        for f in range(8):
            cols = pl.ds(f * 256, 256)
            right = jnp.concatenate([wgt[u, w + 1, g * 2 + f % 2, f // 2] for w, g in pieces], axis=1)
            total = dot_nt(left, right)
            for i, p in enumerate(places):
                block = total[i * 256 : i * 256 + 256].reshape(2, 128, 256)
                if u:
                    block = block + dn[p, :, :, cols].astype(F32)
                dn[p, :, :, cols] = block.astype(BF)

    def d_cross(k):
        net.start(("cross", k), "dn", dn.at[xp(k), 1 - c], dn_sib.at[xp(k)], sib)

    def add_rows(dst, src, n):
        @pl.loop(0, n // 16)
        def _(m):
            rows = pl.ds(pl.multiple_of(m * 16, 16), 16)
            dst[rows, :] = (dst[rows, :].astype(F32) + src[rows, :].astype(F32)).astype(BF)

    def d_merge(k):
        arrived(("cross", k), dn_sib.at[xp(k)])
        add_rows(dn.at[xp(k), c], dn_sib.at[xp(k)], 128)

    d_ring = (
        "dx",
        lambda k, h: dn.at[xp(k), c, pl.ds(h * 64, 64)],
        lambda s: far_x.at[s],
        lambda s, h: near_x.at[s, pl.ds(h * 64, 64)],
        to_x,
        "dn",
    )

    def d_inputs():
        arrived("dx", near_x)

        @pl.loop(0, 8)
        def _(m):
            rows = pl.ds(pl.multiple_of(m * 16, 16), 16)
            unit, inv = norm_rows(m)
            d_normed = dn[x, c, rows, :].astype(F32) + near_x[0, rows, :].astype(F32) + near_x[1, rows, :].astype(F32)
            d_unit = d_normed * gain_ref[...]
            branch = inv * (d_unit - unit * jnp.mean(d_unit * unit, axis=-1, keepdims=True))
            dx_ref[rows, :] = (cot[x, c, rows, :].astype(F32) + branch).astype(BF)

    def d_add(dst, src):
        add_rows(dst, src, 64)

    loaded(2, rb_ref)
    rel[zh] = jnp.zeros((8, 128), F32)
    rel[zh, 0:4, 0:32] = rb_ref[...]
    loaded(0, x_ref)
    loaded(1, gain_ref)
    normalize()
    loaded(3, cot.at[x, c])
    loaded(4, wgt.at[pl.ds(0, 2), pl.ds(0, 4), z, y])
    pl.semaphore_wait(barrier, len(peers))
    weights_a(0)
    tokens_a("cot", cot)
    tokens_a("tok", tok)
    net.start("rel", "rel", rel.at[zh], rel.at[zh], to_z[2])
    weights_b(0)
    weights_a(1)
    weights_c(0)
    weights_b(1)
    spread_bias()
    weights_d(0)
    tokens_b("cot", cot)
    weights_c(1)
    tokens_b("tok", tok)
    weights_here(0)
    arrived("own", tok.at[pl.ds(0, 2), 0])
    passages(0, [x])
    arrived("near", tok.at[pl.ds(0, 4), 0])
    tokens_c("cot", cot)
    passages(0, [xp(1)])
    weights_d(1)
    tokens_c("tok", tok)
    passages(0, [xp(3)])
    arrived("far", tok.at[pl.ds(0, 2), 0])
    passages(0, [xp(2)])
    weight_grads(0, 2)
    grads_far(0)
    for k in (1, 3):
        weight_grads(0, k)
        grads_next(0, k)
    d_tokens(0, [xp(2), xp(1), xp(3)])
    weights_here(1)
    passages(1, [0, 1])
    grads_b(0)
    passages(1, [2, 3])
    weight_grads(1, 2)
    grads_far(1)
    d_tokens(1, [xp(2)])
    d_cross(2)
    for k in (1, 3):
        weight_grads(1, k)
        grads_next(1, k)
    d_merge(2)
    ring_far(*d_ring)
    d_tokens(1, [xp(1), xp(3)])
    d_cross(1)
    d_cross(3)
    weight_grads(0, 0)
    d_merge(1)
    ring_near(1, "dx", *d_ring)
    d_merge(3)
    ring_near(3, "dx", *d_ring)
    grads_c(0, 0)
    grads_b(1)
    weight_grads(1, 0)
    for k in (1, 3):
        ring_add(k, d_add, *d_ring)
        ring_both(k, "dx", *d_ring)
    d_tokens(0, [x])
    d_tokens(1, [x])
    d_cross(0)
    d_merge(0)
    grads_c(1, 0)
    grads_near(1, 0)
    grads_near(0, 0)
    grads_c(1, 1)
    grads_near(1, 1)
    grads_d(1, 0)
    grads_d(0, 0)
    grads_d(1, 1)
    d_inputs()
    grads_e(0)
    grads_e(1)
    w_all = wgt.at[pl.ds(0, 2), pl.ds(0, 4), pl.ds(0, 4), pl.ds(0, 4), pl.ds(0, 240)]
    rows_all = tok.at[pl.ds(0, 4), pl.ds(0, 2), pl.ds(0, 112)]
    sizes = {"w": w_all, "cot": rows_all, "tok": rows_all, "rel": rel.at[zh], "sums": w_all, "dn": rows_all}
    assert len(net.groups) == N_GROUPS and len(net.sends) == N_SENDS
    for name, ref in sizes.items():
        net.sent(name, ref, sib)


def write_results(*refs):
    n = len(refs) // 2
    copies = [pltpu.make_async_copy(refs[i], refs[n + i], refs[-1].at[i]) for i in range(n)]
    for copy in copies:
        copy.start()
    for copy in copies:
        copy.wait()


def per_device(inputs, gain, w_query, w_key, w_value, w_out, rel_bias, d_output):
    vmem, anywhere = pl.BlockSpec(memory_space=pltpu.VMEM), pl.BlockSpec(memory_space=pl.ANY)
    grad = jax.ShapeDtypeStruct((256, 256), F32)
    shapes = (jax.ShapeDtypeStruct((128, 2048), BF), grad, grad, grad, grad)
    results = pl.pallas_call(
        kernel,
        out_shape=tuple(pltpu.VMEM(s.shape, s.dtype) for s in shapes),
        in_specs=[anywhere] * 8,
        out_specs=(vmem,) * 5,
        scratch_shapes=[
            pltpu.VMEM((4, 2, 128, 2048), BF),
            pltpu.VMEM((4, 2, 128, 2048), BF),
            pltpu.VMEM((2, 4, 4, 4, 256, 128), BF),
            pltpu.VMEM((2, 8, 128), F32),
            pltpu.VMEM((8, 256, 256), F32),
            pltpu.VMEM((4, 1024, 256), BF),
            pltpu.VMEM((2, 3, 1024, 256), BF),
            pltpu.VMEM((2, 4, 256, 1024), BF),
            pltpu.VMEM((2, 4, 2, 2, 2, 2, 64, 256), BF),
            pltpu.VMEM((2, 4, 2, 2, 4, 64, 256), BF),
            pltpu.VMEM((2, 2, 2, 2, 2, 64, 256), BF),
            pltpu.VMEM((2, 2, 2, 4, 64, 256), BF),
            pltpu.VMEM((2, 2, 2, 2, 2, 2, 64, 256), BF),
            pltpu.VMEM((2, 2, 2, 2, 4, 64, 256), BF),
            pltpu.VMEM((2, 2, 2, 2, 64, 256), BF),
            pltpu.VMEM((2, 2, 2, 2, 2, 64, 256), BF),
            pltpu.VMEM((4, 2, 128, 2048), BF),
            pltpu.VMEM((4, 128, 2048), BF),
            pltpu.VMEM((2, 64, 2048), BF),
            pltpu.VMEM((2, 128, 2048), BF),
            pltpu.VMEM((32, 8, 128), F32),
            pltpu.VMEM((128, 2048), BF),
            pltpu.VMEM((1, 2048), F32),
            pltpu.VMEM((4, 32), F32),
            pltpu.SemaphoreType.DMA((N_SENDS,)),
            pltpu.SemaphoreType.DMA((N_GROUPS,)),
            pltpu.SemaphoreType.DMA((5,)),
        ],
        compiler_params=pltpu.CompilerParams(
            collective_id=0, has_side_effects=True, vmem_limit_bytes=60 * 1024 * 1024
        ),
        name="attention_backward",
    )(inputs, gain.reshape(1, -1), w_query, w_key, w_value, w_out, rel_bias, d_output)
    return pl.pallas_call(
        write_results,
        out_shape=shapes,
        in_specs=[vmem] * 5,
        out_specs=(anywhere,) * 5,
        scratch_shapes=[pltpu.SemaphoreType.DMA((5,))],
        compiler_params=pltpu.CompilerParams(vmem_limit_bytes=8 * 1024 * 1024),
        name="write_results",
    )(*results)


def solution(mesh):
    return jax.shard_map(
        per_device,
        mesh=mesh,
        in_specs=(
            P(("fsdp", "tensor"), None),
            P(),
            P("fsdp", "tensor"),
            P("fsdp", "tensor"),
            P("fsdp", "tensor"),
            P("fsdp", "tensor"),
            P("tensor", None),
            P(("fsdp", "tensor"), None),
        ),
        out_specs=(
            P(("fsdp", "tensor"), None),
            P("fsdp", "tensor"),
            P("fsdp", "tensor"),
            P("fsdp", "tensor"),
            P("fsdp", "tensor"),
        ),
        check_vma=False,
    )
```

```python
import functools

import jax
import jax.numpy as jnp
import numpy as np
from jax import lax
from jax.experimental import pallas as pl
from jax.experimental.pallas import tpu as pltpu
from jax.sharding import PartitionSpec as P

BUCKETS = 32
MAX_DIST = 128
LEN = 256
EPSILON = 1e-06
MESH = pl.DeviceIdType.MESH
BF = jnp.bfloat16
F32 = jnp.float32
OUT, VAL, QRY, KEY = 0, 1, 2, 3


def bucket_steps():
    half_count = BUCKETS // 2
    exact_count = half_count // 2
    distance = np.arange(LEN)
    log_ratio = np.log(np.maximum(distance, 1) / exact_count) / np.log(MAX_DIST / exact_count)
    far = np.minimum(
        exact_count + np.floor(log_ratio * (half_count - exact_count)).astype(np.int64),
        half_count - 1,
    )
    bucket = np.where(distance < exact_count, distance, far)
    return [int(np.argmax(bucket >= k)) for k in range(half_count)]


def dot_nn(a, b):
    return lax.dot_general(a, b, (((1,), (0,)), ((), ())), preferred_element_type=F32)


def dot_nt(a, b):
    return lax.dot_general(a, b, (((1,), (1,)), ((), ())), preferred_element_type=F32)


class Links:
    def __init__(self, send_sem, recv_sem):
        self.send_sem, self.recv_sem = send_sem, recv_sem
        self.groups = {}
        self.sends = {}

    def start(self, group, send, src, dst, peer):
        k = self.groups.setdefault(group, len(self.groups))
        j = self.sends.setdefault(send, len(self.sends))
        pltpu.make_async_remote_copy(
            src_ref=src,
            dst_ref=dst,
            send_sem=self.send_sem.at[j],
            recv_sem=self.recv_sem.at[k],
            device_id=peer,
            device_id_type=MESH,
        ).start()

    def waiter(self, j, k, ref, peer):
        return pltpu.make_async_remote_copy(
            src_ref=ref,
            dst_ref=ref,
            send_sem=self.send_sem.at[j],
            recv_sem=self.recv_sem.at[k],
            device_id=peer,
            device_id_type=MESH,
        )

    def arrived(self, group, ref, peer):
        self.waiter(0, self.groups[group], ref, peer).wait_recv()

    def sent(self, send, ref, peer):
        self.waiter(self.sends[send], 0, ref, peer).wait_send()


N_GROUPS, N_SENDS = 75, 6


def kernel(
    x_in, gain_in, wq_in, wk_in, wv_in, wo_in, rb_in, do_in,
    dx_ref, gq_ref, gk_ref, gv_ref, go_ref,
    tok, cot, wgt, rel, bias, heads, dheads, rows_t,
    part_y, part_z, far_y, far_z, near_y, near_z, far2, near2,
    dn, dn_sib, far_x, near_x, splat, x_ref, gain_ref, rb_ref, send_sem, recv_sem, load_sem,
):
    f, t = lax.axis_index("fsdp"), lax.axis_index("tensor")
    x, zh, c = t // 4, (t // 2) % 2, t % 2
    y, zl = f // 2, f % 2
    z = zh * 2 + zl

    def dev(x, y, z, c):
        return (y * 2 + z % 2, (x * 2 + z // 2) * 2 + c)

    def xp(k):
        return (x + k) % 4

    def yp(k):
        return (y + k) % 4

    def zp(k):
        return (z + k) % 4

    sib = dev(x, y, z, 1 - c)
    to_x = {k: dev(xp(k), y, z, c) for k in (1, 3)}
    to_y = {k: dev(x, yp(k), z, c) for k in (1, 3)}
    to_z = {k: dev(x, y, zp(k), c) for k in (1, 2, 3)}
    peers = [sib] + list(to_x.values()) + list(to_y.values()) + list(to_z.values())
    barrier = pltpu.get_barrier_semaphore()
    for peer in peers:
        pl.semaphore_signal(barrier, inc=1, device_id=peer, device_id_type=MESH)

    loads = [(x_in, x_ref, 0), (gain_in, gain_ref, 1), (rb_in, rb_ref, 2), (do_in, cot.at[x, c], 3)]
    for u in range(2):
        for w, ref in ((OUT, wo_in), (VAL, wv_in), (QRY, wq_in), (KEY, wk_in)):
            loads.append((ref.at[:, pl.ds(u * 128, 128)], wgt.at[u, w, z, y], 4))
    for src, dst, i in loads:
        pltpu.make_async_copy(src, dst, load_sem.at[i]).start()

    def loaded(i, ref):
        pltpu.make_async_copy(ref, ref, load_sem.at[i]).wait()

    net = Links(send_sem, recv_sem)

    def chunk(u, zz, yy, row, n):
        return wgt.at[u, pl.ds(0, 4), zz, yy, pl.ds(row, n)]

    def column(u, zz, row, n):
        return wgt.at[u, pl.ds(0, 4), zz, pl.ds(0, 4), pl.ds(row, n)]

    def line(u, yy, row, n):
        return wgt.at[u, pl.ds(0, 4), pl.ds(0, 4), yy, pl.ds(row, n)]

    def arrived(group, ref):
        net.arrived(group, ref, sib)

    def weights_a(u):
        for part in range(2):
            for k, row in ((1, part * 64), (3, 64 - part * 64)):
                for name, to, at in (("y", to_y, 0), ("z", to_z, 128)):
                    s = chunk(u, z, y, at + row, 64)
                    net.start((name, u) if part else (name, u, k), "w", s, s, to[k])

    def weights_b(u):
        for k, row in ((1, 0), (3, 64)):
            s = chunk(u, z, yp(4 - k), row, 64)
            arrived(("y", u, k), s)
            net.start(("y", u), "w", s, s, to_y[k])
            s = chunk(u, zp(4 - k), y, 128 + row, 64)
            arrived(("z", u, k), s)
            net.start(("z", u), "w", s, s, to_z[k])

    def weights_c(u):
        arrived(("y", u), column(u, z, 0, 64))
        for part in range(2):
            for k, row in ((1, part * 64), (3, 64 - part * 64)):
                s = column(u, z, row, 64)
                net.start(("all", u) if part else ("z2", u, k), "w", s, s, to_z[k])
        arrived(("z", u), line(u, y, 128, 64))
        for part in range(2):
            for k, row in ((1, part * 64), (3, 64 - part * 64)):
                s = line(u, y, 128 + row, 64)
                net.start(("all", u) if part else ("y2", u, k), "w", s, s, to_y[k])

    def weights_d(u):
        for k, row in ((1, 0), (3, 64)):
            s = column(u, zp(4 - k), row, 64)
            arrived(("z2", u, k), s)
            net.start(("all", u), "w", s, s, to_z[k])
            s = line(u, yp(4 - k), 128 + row, 64)
            arrived(("y2", u, k), s)
            net.start(("all", u), "w", s, s, to_y[k])

    def weights_here(u):
        arrived(("all", u), wgt.at[u, pl.ds(0, 4), pl.ds(0, 4), pl.ds(0, 4), pl.ds(0, 128)])

    def tokens_a(name, buf):
        for k in (1, 3):
            net.start((name, k), name, buf.at[x, c], buf.at[x, c], to_x[k])
        net.start("own", name, buf.at[x, c], buf.at[x, c], sib)

    def tokens_b(name, buf):
        for k, row in ((1, 0), (3, 64)):
            arrived((name, k), buf.at[xp(4 - k), c])
            s = buf.at[xp(4 - k), c, pl.ds(row, 64)]
            net.start((name, "far"), name, s, s, to_x[k])
            s = buf.at[xp(4 - k), c]
            net.start("near", name, s, s, sib)

    def tokens_c(name, buf):
        s = buf.at[xp(2), c]
        arrived((name, "far"), s)
        net.start("far", name, s, s, sib)

    def norm_rows(k):
        rows = x_ref[pl.ds(pl.multiple_of(k * 16, 16), 16), :].astype(F32)
        inv = lax.rsqrt(jnp.mean(rows * rows, axis=-1, keepdims=True) + EPSILON)
        return rows * inv, inv

    def normalize():
        @pl.loop(0, 8)
        def _(k):
            unit, _ = norm_rows(k)
            tok[x, c, pl.ds(pl.multiple_of(k * 16, 16), 16), :] = (unit * gain_ref[...]).astype(BF)

    def spread_bias():
        arrived("rel", rel.at[zh])
        steps = bucket_steps()
        table = jnp.concatenate([rel[0, 0:4, :], rel[1, 0:4, :]], axis=0)
        for k in range(BUCKETS):
            splat[k] = jnp.broadcast_to(table[:, k : k + 1], (8, 128))

        @pl.loop(0, LEN // 8)
        def _(k):
            i = lax.broadcasted_iota(jnp.int32, (8, LEN), 0) + k * 8
            r = lax.broadcasted_iota(jnp.int32, (8, LEN), 1) - i

            def row(b, h):
                return jnp.broadcast_to(splat[b, h : h + 1, 0:1], (8, LEN))

            values = [row(0, h) for h in range(8)]
            for b in range(1, BUCKETS // 2):
                for chosen, at in ((r <= -steps[b], b), (r >= steps[b], BUCKETS // 2 + b)):
                    for h in range(8):
                        values[h] = jnp.where(chosen, row(at, h), values[h])
            for h in range(8):
                bias[h, pl.ds(pl.multiple_of(k * 8, 8), 8), :] = values[h]

    lane = lax.broadcasted_iota(jnp.int32, (1, 128), 1)
    mask = [(lane < 64).astype(F32).astype(BF), (lane >= 64).astype(F32).astype(BF)]
    row_at = lax.broadcasted_iota(jnp.int32, (128, 1), 0)
    mask_t = [(row_at < 64).astype(F32).astype(BF), (row_at >= 64).astype(F32).astype(BF)]

    def passages(u, places):
        n = len(places)

        def by_chunk(buf):
            whole = jnp.concatenate([buf[p].reshape(256, 2048) for p in places], axis=0)
            order = [yy * 2 + zz for zz in range(2) for yy in range(4)]
            return jnp.concatenate([whole[:, i * 256 : i * 256 + 256] for i in order], axis=1)

        for w in range(4):
            left = by_chunk(cot if w == OUT else tok)
            right = jnp.concatenate([wgt[u, w, g * 2 : g * 2 + 2].reshape(2048, 128) for g in range(2)], axis=1)
            heads[w, 0 : n * 256] = dot_nn(left, right).astype(BF)
        for i, p in enumerate(places):
            attention(u, i, pl.ds(pl.multiple_of(p * 256, 256), 256))

    def attention(u, i, rows):
        parts = [
            tuple(heads[w, i * 256 : i * 256 + 256, g * 128 : g * 128 + 128] for w in range(4)) for g in range(2)
        ]
        scores = [
            [dot_nt(q2 * mask[h], k2) + bias[g * 4 + u * 2 + h] for h in range(2)]
            for g, (_, _, q2, k2) in enumerate(parts)
        ]
        d_prob = [[dot_nt(dc2 * mask[h], v2) for h in range(2)] for dc2, v2, _, _ in parts]
        probs_b, d_score = [[], []], [[], []]
        for g in range(2):
            for h in range(2):
                e = jnp.exp(scores[g][h] - jnp.max(scores[g][h], axis=-1, keepdims=True))
                probs = e * (1.0 / jnp.sum(e, axis=-1, keepdims=True))
                row_dot = jnp.sum(probs * d_prob[g][h], axis=-1, keepdims=True)
                probs_b[g].append(probs.astype(BF))
                d_score[g].append((probs * (d_prob[g][h] - row_dot)).astype(BF))
        for g, (dc2, v2, q2, k2) in enumerate(parts):
            ctx = dot_nn(
                jnp.concatenate(probs_b[g], axis=1),
                jnp.concatenate([v2 * mask[0], v2 * mask[1]], axis=0),
            ).astype(BF)
            dq = dot_nn(
                jnp.concatenate(d_score[g], axis=1),
                jnp.concatenate([k2 * mask[0], k2 * mask[1]], axis=0),
            ).astype(BF)
            dc_t, q_t = dc2.T, q2.T
            dv_t = dot_nn(
                jnp.concatenate([dc_t * mask_t[0], dc_t * mask_t[1]], axis=1),
                jnp.concatenate(probs_b[g], axis=0),
            ).astype(BF)
            dk_t = dot_nn(
                jnp.concatenate([q_t * mask_t[0], q_t * mask_t[1]], axis=1),
                jnp.concatenate(d_score[g], axis=0),
            ).astype(BF)
            at, lanes = pl.ds(g * 128, 128), pl.ds(g * 128, 128)
            rows_t[u, OUT, at, rows] = ctx.T
            rows_t[u, VAL, at, rows] = dv_t
            rows_t[u, QRY, at, rows] = dq.T
            rows_t[u, KEY, at, rows] = dk_t
            dheads[u, VAL - 1, rows, lanes] = dv_t.T
            dheads[u, QRY - 1, rows, lanes] = dq
            dheads[u, KEY - 1, rows, lanes] = dk_t.T

    def weight_grads(u, k):
        weight_grads_y(u, k)
        weight_grads_z(u, k)

    def weight_grads_y(u, k):
        cols = pl.ds(pl.multiple_of(yp(k) * 512, 512), 512)
        for w, buf in ((OUT, cot), (VAL, tok)):
            res = dot_nn(rows_t[u, w], buf[:, :, :, cols].reshape(1024, 512)).astype(BF)
            for g in range(2):
                for h in range(2):
                    at = g * 128 + h * 64
                    for fz in range(2):
                        part_y[u, yp(k), h, w, g, fz] = res[at : at + 64, fz * 256 : fz * 256 + 256]

    def weight_grads_z(u, k):
        rows = pl.ds(pl.multiple_of(zp(k) // 2 * 128, 128), 128)
        left = jnp.concatenate([rows_t[u, w, rows] for w in (QRY, KEY)], axis=0)
        starts = [pl.multiple_of((fy * 2 + zp(k) % 2) * 256, 256) for fy in range(4)]
        right = jnp.concatenate([tok[:, :, :, pl.ds(at, 256)].reshape(1024, 256) for at in starts], axis=1)
        res = dot_nn(left, right).astype(BF)
        for w in range(2):
            for h in range(2):
                at = w * 128 + h * 64
                for fy in range(4):
                    part_z[u, zp(k), h, w, fy] = res[at : at + 64, fy * 256 : fy * 256 + 256]

    def ring_far(key, block, far, near, to, send):
        net.start((key, "far", 1), send, block(2, 0), far(0), to[1])
        net.start((key, "far", 3), send, block(2, 1), far(1), to[3])

    def ring_near(k, group, key, block, far, near, to, send):
        half, side = (1, 0) if k == 1 else (0, 1)
        net.start(group, send, block(k, half), near(side, half), to[k])

    def ring_both(k, group, key, block, far, near, to, send):
        half, side = (0, 0) if k == 1 else (1, 1)
        net.start(group, send, block(k, half), near(side, half), to[k])

    def ring_add(k, add, key, block, far, near, to, send):
        half, side = (0, 0) if k == 1 else (1, 1)
        arrived((key, "far", k), far(side))
        add(block(k, half), far(side))

    def add_into(dst, src):
        dst[...] = (dst[...].astype(F32) + src[...].astype(F32)).astype(BF)

    def add_each(dst, src):
        for w in range(dst.shape[0]):
            add_into(dst.at[w], src.at[w])

    splits = {0: [(0, 2)], 1: [(0, 1), (1, 1)]}

    def first(u, pair, start=0, n=2):
        ws = pl.ds(start, n)
        if pair == 0:
            return (
                ("s1", u, pair),
                lambda k, h: part_y.at[u, yp(k), h, ws],
                lambda s: far_y.at[u, s, ws],
                lambda s, h: near_y.at[u, s, h, ws],
                to_y,
                "sums",
            )
        return (
            ("s1", u, pair),
            lambda k, h: part_z.at[u, zp(k), h, ws],
            lambda s: far_z.at[u, s, ws],
            lambda s, h: near_z.at[u, s, h, ws],
            to_z,
            "sums",
        )

    def second(u, pair, start, n):
        ws = pl.ds(start, n)

        def block(k, h):
            if pair == 0:
                return part_y.at[u, y, h, ws, zp(k) // 2, zp(k) % 2]
            return part_z.at[u, z, h, ws, yp(k)]

        return (
            ("s2", u, pair, start),
            block,
            lambda s: far2.at[u, pair, s, ws],
            lambda s, h: near2.at[u, pair, s, h, ws],
            to_z if pair == 0 else to_y,
            "sums",
        )

    def grads_far(u):
        weight_grads_y(u, 2)
        ring_far(*first(u, 0))
        weight_grads_z(u, 2)
        ring_far(*first(u, 1))

    def grads_next(u, k):
        for pair in range(2):
            ring_near(k, ("s1n", u, pair), *first(u, pair))

    def grads_b(u):
        for k in (1, 3):
            for pair in range(2):
                ring_add(k, add_each, *first(u, pair))
                start, n = splits[u][0]
                ring_both(k, ("s1b", u, pair, start), *first(u, pair, start, n))
        for start, n in splits[u][1:]:
            for k in (1, 3):
                for pair in range(2):
                    ring_both(k, ("s1b", u, pair, start), *first(u, pair, start, n))

    def grads_c(u, part):
        start, n = splits[u][part]
        for pair in range(2):
            own, near = (part_y.at[u, y], near_y.at[u]) if pair == 0 else (part_z.at[u, z], near_z.at[u])
            if part == 0:
                arrived(("s1n", u, pair), near.at[0])
            arrived(("s1b", u, pair, start), near.at[0] if n == 2 else near.at[0, 0])
            for h in range(2):
                for w in range(start, start + n):
                    total = own[h, w].astype(F32) + near[0, h, w].astype(F32) + near[1, h, w].astype(F32)
                    own[h, w] = total.astype(BF)
            ring_far(*second(u, pair, start, n))

    def grads_near(u, part):
        for pair in range(2):
            for k in (1, 3):
                args = second(u, pair, *splits[u][part])
                ring_near(k, args[0], *args)

    def grads_d(u, part):
        for k in (1, 3):
            for pair in range(2):
                args = second(u, pair, *splits[u][part])
                ring_add(k, add_into, *args)
                ring_both(k, args[0], *args)

    def grads_e(u):
        for pair, outs in ((0, (go_ref, gv_ref)), (1, (gq_ref, gk_ref))):
            near = near2.at[u, pair]
            for start, n in splits[u]:
                arrived(("s2", u, pair, start), near if n == 2 else near.at[0])
            for w in range(2):
                for h in range(2):
                    own = part_y[u, y, h, w, zh, zl] if pair == 0 else part_z[u, z, h, w, y]
                    total = own.astype(F32) + near[0, h, w].astype(F32) + near[1, h, w].astype(F32)
                    outs[w][:, u * 128 + h * 64 : u * 128 + h * 64 + 64] = total.T

    def d_tokens(u, places):
        pieces = [(w, g) for w in range(3) for g in range(2)]
        left = jnp.concatenate(
            [
                jnp.concatenate([dheads[u, w, pl.ds(pl.multiple_of(p * 256, 256), 256), :] for w in range(3)], axis=1)
                for p in places
            ],
            axis=0,
        )
        for f in range(8):
            cols = pl.ds(f * 256, 256)
            right = jnp.concatenate([wgt[u, w + 1, g * 2 + f % 2, f // 2] for w, g in pieces], axis=1)
            total = dot_nt(left, right)
            for i, p in enumerate(places):
                block = total[i * 256 : i * 256 + 256].reshape(2, 128, 256)
                if u:
                    block = block + dn[p, :, :, cols].astype(F32)
                dn[p, :, :, cols] = block.astype(BF)

    def d_cross(k):
        net.start(("cross", k), "dn", dn.at[xp(k), 1 - c], dn_sib.at[xp(k)], sib)

    def add_rows(dst, src, n):
        @pl.loop(0, n // 16)
        def _(m):
            rows = pl.ds(pl.multiple_of(m * 16, 16), 16)
            dst[rows, :] = (dst[rows, :].astype(F32) + src[rows, :].astype(F32)).astype(BF)

    def d_merge(k):
        arrived(("cross", k), dn_sib.at[xp(k)])
        add_rows(dn.at[xp(k), c], dn_sib.at[xp(k)], 128)

    d_ring = (
        "dx",
        lambda k, h: dn.at[xp(k), c, pl.ds(h * 64, 64)],
        lambda s: far_x.at[s],
        lambda s, h: near_x.at[s, pl.ds(h * 64, 64)],
        to_x,
        "dn",
    )

    def d_inputs():
        arrived("dx", near_x)

        @pl.loop(0, 8)
        def _(m):
            rows = pl.ds(pl.multiple_of(m * 16, 16), 16)
            unit, inv = norm_rows(m)
            d_normed = dn[x, c, rows, :].astype(F32) + near_x[0, rows, :].astype(F32) + near_x[1, rows, :].astype(F32)
            d_unit = d_normed * gain_ref[...]
            branch = inv * (d_unit - unit * jnp.mean(d_unit * unit, axis=-1, keepdims=True))
            dx_ref[rows, :] = (cot[x, c, rows, :].astype(F32) + branch).astype(BF)

    def d_add(dst, src):
        add_rows(dst, src, 64)

    loaded(2, rb_ref)
    rel[zh] = jnp.zeros((8, 128), F32)
    rel[zh, 0:4, 0:32] = rb_ref[...]
    loaded(0, x_ref)
    loaded(1, gain_ref)
    normalize()
    loaded(3, cot.at[x, c])
    loaded(4, wgt.at[pl.ds(0, 2), pl.ds(0, 4), z, y])
    pl.semaphore_wait(barrier, len(peers))
    weights_a(0)
    tokens_a("cot", cot)
    tokens_a("tok", tok)
    net.start("rel", "rel", rel.at[zh], rel.at[zh], to_z[2])
    weights_b(0)
    weights_a(1)
    weights_c(0)
    weights_b(1)
    spread_bias()
    weights_d(0)
    tokens_b("cot", cot)
    weights_c(1)
    tokens_b("tok", tok)
    weights_here(0)
    arrived("own", tok.at[pl.ds(0, 2), 0])
    passages(0, [x])
    arrived("near", tok.at[pl.ds(0, 4), 0])
    tokens_c("cot", cot)
    passages(0, [xp(1)])
    weights_d(1)
    tokens_c("tok", tok)
    passages(0, [xp(3)])
    arrived("far", tok.at[pl.ds(0, 2), 0])
    passages(0, [xp(2)])
    grads_far(0)
    for k in (1, 3):
        weight_grads(0, k)
        grads_next(0, k)
    d_tokens(0, [xp(2), xp(1), xp(3)])
    weights_here(1)
    passages(1, [0, 1])
    grads_b(0)
    passages(1, [2, 3])
    grads_far(1)
    d_tokens(1, [xp(2)])
    d_cross(2)
    for k in (1, 3):
        weight_grads(1, k)
        grads_next(1, k)
    d_merge(2)
    ring_far(*d_ring)
    d_tokens(1, [xp(1), xp(3)])
    d_cross(1)
    d_cross(3)
    weight_grads(0, 0)
    d_merge(1)
    ring_near(1, "dx", *d_ring)
    d_merge(3)
    ring_near(3, "dx", *d_ring)
    grads_c(0, 0)
    grads_b(1)
    weight_grads(1, 0)
    for k in (1, 3):
        ring_add(k, d_add, *d_ring)
        ring_both(k, "dx", *d_ring)
    d_tokens(0, [x])
    d_tokens(1, [x])
    d_cross(0)
    d_merge(0)
    grads_c(1, 0)
    grads_near(1, 0)
    grads_near(0, 0)
    grads_c(1, 1)
    grads_near(1, 1)
    grads_d(1, 0)
    grads_d(0, 0)
    grads_d(1, 1)
    d_inputs()
    grads_e(0)
    grads_e(1)
    w_all = wgt.at[pl.ds(0, 2), pl.ds(0, 4), pl.ds(0, 4), pl.ds(0, 4), pl.ds(0, 240)]
    rows_all = tok.at[pl.ds(0, 4), pl.ds(0, 2), pl.ds(0, 112)]
    sizes = {"w": w_all, "cot": rows_all, "tok": rows_all, "rel": rel.at[zh], "sums": w_all, "dn": rows_all}
    assert len(net.groups) == N_GROUPS and len(net.sends) == N_SENDS
    for name, ref in sizes.items():
        net.sent(name, ref, sib)


def write_results(*refs):
    n = len(refs) // 2
    copies = [pltpu.make_async_copy(refs[i], refs[n + i], refs[-1].at[i]) for i in range(n)]
    for copy in copies:
        copy.start()
    for copy in copies:
        copy.wait()


def per_device(inputs, gain, w_query, w_key, w_value, w_out, rel_bias, d_output):
    vmem, anywhere = pl.BlockSpec(memory_space=pltpu.VMEM), pl.BlockSpec(memory_space=pl.ANY)
    grad = jax.ShapeDtypeStruct((256, 256), F32)
    shapes = (jax.ShapeDtypeStruct((128, 2048), BF), grad, grad, grad, grad)
    results = pl.pallas_call(
        kernel,
        out_shape=tuple(pltpu.VMEM(s.shape, s.dtype) for s in shapes),
        in_specs=[anywhere] * 8,
        out_specs=(vmem,) * 5,
        scratch_shapes=[
            pltpu.VMEM((4, 2, 128, 2048), BF),
            pltpu.VMEM((4, 2, 128, 2048), BF),
            pltpu.VMEM((2, 4, 4, 4, 256, 128), BF),
            pltpu.VMEM((2, 8, 128), F32),
            pltpu.VMEM((8, 256, 256), F32),
            pltpu.VMEM((4, 1024, 256), BF),
            pltpu.VMEM((2, 3, 1024, 256), BF),
            pltpu.VMEM((2, 4, 256, 1024), BF),
            pltpu.VMEM((2, 4, 2, 2, 2, 2, 64, 256), BF),
            pltpu.VMEM((2, 4, 2, 2, 4, 64, 256), BF),
            pltpu.VMEM((2, 2, 2, 2, 2, 64, 256), BF),
            pltpu.VMEM((2, 2, 2, 4, 64, 256), BF),
            pltpu.VMEM((2, 2, 2, 2, 2, 2, 64, 256), BF),
            pltpu.VMEM((2, 2, 2, 2, 4, 64, 256), BF),
            pltpu.VMEM((2, 2, 2, 2, 64, 256), BF),
            pltpu.VMEM((2, 2, 2, 2, 2, 64, 256), BF),
            pltpu.VMEM((4, 2, 128, 2048), BF),
            pltpu.VMEM((4, 128, 2048), BF),
            pltpu.VMEM((2, 64, 2048), BF),
            pltpu.VMEM((2, 128, 2048), BF),
            pltpu.VMEM((32, 8, 128), F32),
            pltpu.VMEM((128, 2048), BF),
            pltpu.VMEM((1, 2048), F32),
            pltpu.VMEM((4, 32), F32),
            pltpu.SemaphoreType.DMA((N_SENDS,)),
            pltpu.SemaphoreType.DMA((N_GROUPS,)),
            pltpu.SemaphoreType.DMA((5,)),
        ],
        compiler_params=pltpu.CompilerParams(
            collective_id=0, has_side_effects=True, vmem_limit_bytes=60 * 1024 * 1024
        ),
        name="attention_backward",
    )(inputs, gain.reshape(1, -1), w_query, w_key, w_value, w_out, rel_bias, d_output)
    return pl.pallas_call(
        write_results,
        out_shape=shapes,
        in_specs=[vmem] * 5,
        out_specs=(anywhere,) * 5,
        scratch_shapes=[pltpu.SemaphoreType.DMA((5,))],
        compiler_params=pltpu.CompilerParams(vmem_limit_bytes=8 * 1024 * 1024),
        name="write_results",
    )(*results)


def solution(mesh):
    return jax.shard_map(
        per_device,
        mesh=mesh,
        in_specs=(
            P(("fsdp", "tensor"), None),
            P(),
            P("fsdp", "tensor"),
            P("fsdp", "tensor"),
            P("fsdp", "tensor"),
            P("fsdp", "tensor"),
            P("tensor", None),
            P(("fsdp", "tensor"), None),
        ),
        out_specs=(
            P(("fsdp", "tensor"), None),
            P("fsdp", "tensor"),
            P("fsdp", "tensor"),
            P("fsdp", "tensor"),
            P("fsdp", "tensor"),
        ),
        check_vma=False,
    )
```
